128 devices in a mesh: row: 8 (over x, y_hi), col: 16 (over y_lo, z, core).
Axes of the slice: x: 4, y: 4 (y_hi: 2, y_lo: 2; y = y_hi * 2 + y_lo), z: 4, core: 2. Of those that a mesh axis runs over, the one named last changes fastest.
Arguments:
- tokens: bfloat16 [1024, 12288], P('col', 'row'), may hold values from -6 to 6
- w_in: bfloat16 [12288, 49152], P('row', 'col'), may hold values from -0.0546875 to 0.0546875
- b_in: bfloat16 [49152], P('col'), may hold values from -3 to 3
- w_out: bfloat16 [49152, 12288], P('col', 'row'), may hold values from -0.02734375 to 0.02734375
- b_out: bfloat16 [12288], P('row'), may hold values from -3 to 3
Outputs:
- output_rows: float32 [1024, 12288], P('col', 'row')
The draws below stay inside these ranges and needn't reach their ends.
All inputs are finite; a program needn't handle non-finite values.
Results may differ from the reference program's by a relative error of at most 0.0024.
Values may be sent and summed in bfloat16 or wider, within the bound.
A program may use at most 128 MiB of HBM per device.

```python
import jax
import jax.numpy as jnp

D = 12288
FF = 49152
TOKENS = 1024


def block_levels(rng, shape, pieces, least, high):
    def one(axis_at, shards_of):
        steps = jax.random.uniform(jax.random.fold_in(jax.random.fold_in(rng, 6), axis_at), (shards_of,), jnp.float32, least / len(pieces), high / len(pieces))
        return jnp.repeat(jnp.exp(steps), shape[axis_at] // shards_of).reshape((-1,) + (1,) * (len(shape) - axis_at - 1))

    gain = one(*pieces[0])
    for cut in pieces[1:]:
        gain = gain * one(*cut)
    return gain


def scatter_about(own_key, extent, deviation, reach, split=(), dtype=jnp.bfloat16):
    drawn = deviation * jax.random.normal(own_key, extent, jnp.float32)
    if split:
        drawn = drawn * block_levels(own_key, extent, split, -0.22, 0.18)
    return jnp.clip(drawn, -reach, reach).astype(dtype)


def setup_inputs(seed: int = 0) -> dict:
    seeds = jax.random.split(jax.random.key(seed), 6)
    return {
        "tokens": scatter_about(seeds[0], (TOKENS, D), 1.0, 6.0, ((0, 16), (1, 8))),
        "w_in": scatter_about(seeds[1], (D, FF), D ** -0.5, 0.0546875, ((0, 8), (1, 16))),
        "b_in": scatter_about(seeds[2], (FF,), 0.5, 3.0, ((0, 16),)),
        "w_out": scatter_about(seeds[3], (FF, D), FF ** -0.5, 0.02734375, ((0, 16), (1, 8))),
        "b_out": scatter_about(seeds[4], (D,), 0.5, 3.0, ((0, 8),)),
    }


def reference(tokens, w_in, b_in, w_out, b_out):
    summed = jnp.dot(tokens, w_in, preferred_element_type=jnp.float32)
    hidden = jax.nn.gelu(summed + b_in.astype(jnp.float32), approximate=True).astype(jnp.bfloat16)
    result = jnp.dot(hidden, w_out, preferred_element_type=jnp.float32) + b_out.astype(jnp.float32)
    return result
```

```python
import jax
import jax.numpy as jnp
from jax import lax
from jax.experimental import pallas as pl
from jax.experimental.pallas import tpu as pltpu
from jax.sharding import PartitionSpec as P

MESH = pl.DeviceIdType.MESH
F32, BF16 = jnp.float32, jnp.bfloat16
CHUNKS = 8
ROWS, HALF = 128, 64
D, FF = 1536, 3072
PAIR, QUARTER = 768, 384

ORDER = (
    ("first", 0), ("pass_on", -1), ("sum_y", 1), ("gather_x", 2), ("second", 3), ("sum_x", 0),
    ("activate", 1), ("gather_xx", 2), ("send_out", 3), ("cross", 4),
)
STEPS = CHUNKS + 3


def kernel(tok_hbm, w1_hbm, bin_ref, w2_hbm, bout_ref, out_ref,
           w1, w2, tok, x1s, x1r, keep1, x2s, x2r, keep2, ys, yr, keep3, hid, po, cr, osend, orecv, y2s, y2r,
           w1_sem, w2_sem, own_sem, tok_ss, tok_rs, fwd_ss, fwd_rs, first_ss, relay_ss,
           x1_ss, x1_rs, x2_ss, x2_rs, y_ss, y_rs, gy_ss, gy_rs, gx_ss, gx_rs, gxx_ss, gxx_rs,
           c_ss, c_rs, o_ss, o_rs, y2_ss, y2_rs):
    row, col = lax.axis_index("row"), lax.axis_index("col")
    x, yh = row // 2, row % 2
    yl, z, core = col // 8, (col // 2) % 4, col % 2
    x_one = x + 1 - 2 * (x % 2)
    x_three = 3 - x
    one = (x_one * 2 + yh, col)
    three = (x_three * 2 + yh, col)
    across = (x * 2 + 1 - yh, col)
    sibling = (row, col + 1 - 2 * core)
    low = (row, (1 - yl) * 8 + z * 2 + core)

    def along_z(d):
        return (row, yl * 8 + ((z + d) % 4) * 2 + core)

    mine = (((x + 1) // 2) % 2, x // 2)
    q = (x // 2, x % 2)
    pair_of = tuple(h * 2 * PAIR + mine[h] * PAIR for h in (0, 1))
    other_pair = tuple(h * 2 * PAIR + (1 - mine[h]) * PAIR for h in (0, 1))
    quarter_of = tuple(pair_of[h] + q[h] * QUARTER for h in (0, 1))
    my_block = quarter_of[0] * (1 - yh) + quarter_of[1] * yh
    dest1, dest2 = (one, three), (three, one)

    def cols(start, size):
        return pl.ds(pl.multiple_of(start, 128), size)

    def remote(src, dst, ss, rs, dev):
        return pltpu.make_async_remote_copy(src_ref=src, dst_ref=dst, send_sem=ss, recv_sem=rs, device_id=dev, device_id_type=MESH)

    w1_order = (other_pair[0], other_pair[1], pair_of[0], pair_of[1])

    def load_w1(i):
        c = cols(w1_order[i], PAIR)
        return pltpu.make_async_copy(w1_hbm.at[:, c], w1.at[:, c], w1_sem.at[i])

    own_rows = pl.ds(pl.multiple_of(core * HALF, HALF), HALF)
    other_rows = pl.ds(pl.multiple_of((1 - core) * HALF, HALF), HALF)
    own = pltpu.make_async_copy(tok_hbm, tok.at[0, own_rows], own_sem)
    own.start()
    for i in range(4):
        load_w1(i).start()
    load_w2 = pltpu.make_async_copy(w2_hbm, w2, w2_sem)
    load_w2.start()

    barrier = pltpu.get_barrier_semaphore()
    partners = [one, three, across, sibling, low] + [along_z(d) for d in (1, 2, 3)]
    for dev in partners:
        pl.semaphore_signal(barrier, inc=1, device_id=dev, device_id_type=MESH)
    pl.semaphore_wait(barrier, len(partners))

    def token_slot(t):
        return tok.at[t, own_rows]

    def to_sibling(t):
        return remote(token_slot(t), token_slot(t), fwd_ss.at[t], fwd_rs.at[t], sibling)

    def from_sibling(t):
        return remote(tok.at[t, other_rows], tok.at[t, other_rows], fwd_ss.at[t], fwd_rs.at[t], sibling)

    own.wait()
    to_sibling(0).start()
    to_low = remote(token_slot(0), token_slot(1), first_ss.at[0], tok_rs.at[1], low)
    to_low.start()
    to_z = []
    for d in (1, 3, 2):
        copy = remote(token_slot(0), token_slot(4 + d), first_ss.at[d], tok_rs.at[4 + d], along_z(4 - d))
        copy.start()
        to_z.append(copy)

    def relay(d):
        return remote(token_slot(1), token_slot(1 + d), relay_ss.at[d - 1], tok_rs.at[1 + d], along_z(4 - d))

    def pass_on(t):
        remote(token_slot(t), token_slot(t), tok_ss.at[0], tok_rs.at[t], low).wait_recv()
        to_sibling(t).start()

        @pl.when(t == 1)
        def _():
            for d in (1, 3, 2):
                relay(d).start()

    def x1_copy(t, h):
        return remote(x1s.at[t % 2, h], x1r.at[t, h], x1_ss.at[t % 2, h], x1_rs.at[t, h], dest1[h])

    def first(t):
        from_sibling(t).wait_recv()
        for i in range(4):
            h = i % 2

            @pl.when(t == 0)
            def _():
                load_w1(i).wait()

            if i < 2:
                @pl.when(t >= 2)
                def _():
                    x1_copy(t, h).wait_send()

            part = jnp.dot(tok[t], w1[:, cols(w1_order[i], PAIR)], preferred_element_type=F32)
            if i < 2:
                x1s[t % 2, h] = part.astype(BF16)
                x1_copy(t, h).start()
            else:
                keep1[h] = part

    def x2_copy(t, h):
        return remote(x2s.at[t % 2, h], x2r.at[t, h], x2_ss.at[t % 2, h], x2_rs.at[t, h], dest2[h])

    def sum_x(t):
        for h in (0, 1):
            x1_copy(t, h).wait_recv()

            @pl.when(t >= 2)
            def _():
                x2_copy(t, h).wait_send()

            gone = cols((1 - q[h]) * QUARTER, QUARTER)
            x2s[t % 2, h] = (keep1[h, :, gone] + x1r[t, h, :, gone].astype(F32)).astype(BF16)
            x2_copy(t, h).start()
        for h in (0, 1):
            kept = cols(q[h] * QUARTER, QUARTER)
            keep2[h] = keep1[h, :, kept] + x1r[t, h, :, kept].astype(F32)

    def y_copy(t):
        return remote(ys.at[t % 2], yr.at[t], y_ss.at[t % 2], y_rs.at[t], across)

    def sum_y(t):
        for h in (0, 1):
            x2_copy(t, h).wait_recv()

        @pl.when(t >= 2)
        def _():
            y_copy(t).wait_send()

        ys[t % 2] = keep2[1 - yh] + x2r[t, 1 - yh].astype(F32)
        y_copy(t).start()
        keep3[...] = keep2[yh] + x2r[t, yh].astype(F32)

    def hid_copy(t, start, size, ss, rs, dev):
        c = cols(start, size)
        return remote(hid.at[t, :, c], hid.at[t, :, c], ss, rs, dev)

    def gy_copy(t):
        return hid_copy(t, my_block, QUARTER, gy_ss.at[t], gy_rs.at[t], across)

    def gx_copy(t, h):
        return hid_copy(t, quarter_of[h], QUARTER, gx_ss.at[t, h], gx_rs.at[t, h], dest2[h])

    def gxx_copy(t, h):
        return hid_copy(t, pair_of[h], PAIR, gxx_ss.at[t, h], gxx_rs.at[t, h], dest1[h])

    def activate(t):
        y_copy(t).wait_recv()
        c = cols(my_block, QUARTER)
        hid[t, :, c] = jax.nn.gelu(keep3[...] + yr[t] + bin_ref[:, c], approximate=True).astype(BF16)
        gy_copy(t).start()

    def gather_x(t):
        gy_copy(t).wait_recv()
        for h in (0, 1):
            gx_copy(t, h).start()

    def gather_xx(t):
        for h in (0, 1):
            gx_copy(t, h).wait_recv()
            gxx_copy(t, h).start()

    def c_copy(t):
        return remote(po.at[t % 2, other_rows], cr.at[t], c_ss.at[t % 2], c_rs.at[t], sibling)

    def second(t):
        @pl.when(t == 0)
        def _():
            load_w2.wait()

        @pl.when(t >= 2)
        def _():
            c_copy(t).wait_send()

        for h in (0, 1):
            gxx_copy(t, h).wait_recv()
        for i in range(2):
            c = pl.ds(i * PAIR, PAIR)
            po[t % 2, :, c] = jnp.dot(hid[t], w2[:, c], preferred_element_type=F32)
        c_copy(t).start()

    def o_copy(t):
        far = (t + 3) // 4 % 2
        return remote(osend.at[t % 2], orecv.at[t], o_ss.at[t % 2], o_rs.at[t], along_z((t + 3 * far) % 4))

    def send_out(t):
        c_copy(t).wait_recv()

        @pl.when(t < 2)
        def _():
            orecv[t] = po[t % 2, own_rows] + cr[t]

        @pl.when(t >= 2)
        def _():
            @pl.when(t >= 4)
            def _():
                o_copy(t).wait_send()

            osend[t % 2] = po[t % 2, own_rows] + cr[t]
            o_copy(t).start()

    y2_copy = remote(y2s, y2r, y2_ss, y2_rs, low)

    def cross(t):
        @pl.when(t == 4)
        def _():
            for i in (2, 3, 4):
                o_copy(i).wait_recv()
            y2s[...] = (orecv[1] + orecv[2]) + (orecv[3] + orecv[4])
            y2_copy.start()

    tasks = dict(first=first, pass_on=pass_on, sum_x=sum_x, sum_y=sum_y, activate=activate, gather_x=gather_x,
                 gather_xx=gather_xx, second=second, send_out=send_out, cross=cross)

    def step(s, _):
        for name, lag in ORDER:
            t = s - lag

            @pl.when((t >= (1 if name == "pass_on" else 0)) & (t < CHUNKS))
            def _():
                tasks[name](t)

        return 0

    lax.fori_loop(0, STEPS, step, 0)

    for i in (5, 6, 7):
        o_copy(i).wait_recv()
    y2_copy.wait_recv()
    out_ref[...] = (orecv[0] + orecv[5]) + (orecv[6] + orecv[7]) + y2r[...] + bout_ref[...]

    to_low.wait_send()
    for copy in to_z:
        copy.wait_send()
    for d in (1, 2, 3):
        relay(d).wait_send()
    for t in range(CHUNKS):
        to_sibling(t).wait_send()
        gy_copy(t).wait_send()
        for h in (0, 1):
            gx_copy(t, h).wait_send()
            gxx_copy(t, h).wait_send()
    for t in (CHUNKS - 2, CHUNKS - 1):
        for h in (0, 1):
            x1_copy(t, h).wait_send()
            x2_copy(t, h).wait_send()
        y_copy(t).wait_send()
        c_copy(t).wait_send()
        o_copy(t).wait_send()
    y2_copy.wait_send()


def per_device(tokens, w_in, b_in, w_out, b_out):
    any_space, vmem = pl.BlockSpec(memory_space=pl.ANY), pl.BlockSpec(memory_space=pltpu.VMEM)
    dma = pltpu.SemaphoreType.DMA
    n = CHUNKS
    scratch = [
        pltpu.VMEM((D, FF), BF16), pltpu.VMEM((FF, D), BF16), pltpu.VMEM((n, ROWS, D), BF16),
        pltpu.VMEM((2, 2, ROWS, PAIR), BF16), pltpu.VMEM((n, 2, ROWS, PAIR), BF16), pltpu.VMEM((2, ROWS, PAIR), F32),
        pltpu.VMEM((2, 2, ROWS, QUARTER), BF16), pltpu.VMEM((n, 2, ROWS, QUARTER), BF16), pltpu.VMEM((2, ROWS, QUARTER), F32),
        pltpu.VMEM((2, ROWS, QUARTER), F32), pltpu.VMEM((n, ROWS, QUARTER), F32), pltpu.VMEM((ROWS, QUARTER), F32),
        pltpu.VMEM((n, ROWS, FF), BF16),
        pltpu.VMEM((2, ROWS, D), F32), pltpu.VMEM((n, HALF, D), F32),
        pltpu.VMEM((2, HALF, D), F32), pltpu.VMEM((n, HALF, D), F32),
        pltpu.VMEM((HALF, D), F32), pltpu.VMEM((HALF, D), F32),
        dma((4,)), dma, dma, dma((1,)), dma((n,)), dma((n,)), dma((n,)), dma((4,)), dma((3,)),
        dma((2, 2)), dma((n, 2)), dma((2, 2)), dma((n, 2)), dma((2,)), dma((n,)),
        dma((n,)), dma((n,)), dma((n, 2)), dma((n, 2)), dma((n, 2)), dma((n, 2)),
        dma((2,)), dma((n,)), dma((2,)), dma((n,)), dma, dma,
    ]
    return pl.pallas_call(
        kernel,
        out_shape=jax.ShapeDtypeStruct((HALF, D), F32),
        in_specs=[any_space, any_space, vmem, any_space, vmem],
        out_specs=vmem,
        scratch_shapes=scratch,
        compiler_params=pltpu.CompilerParams(collective_id=0, has_side_effects=True, vmem_limit_bytes=60 * 2**20),
        cost_estimate=pl.CostEstimate(flops=4 * 1024 * D * FF, bytes_accessed=4 * D * FF, transcendentals=1024 * QUARTER),
    )(tokens, w_in, b_in.astype(F32).reshape(1, FF), w_out, b_out.astype(F32).reshape(1, D))


def solution(mesh):
    return jax.shard_map(
        per_device,
        mesh=mesh,
        in_specs=(P("col", "row"), P("row", "col"), P("col"), P("col", "row"), P("row")),
        out_specs=P("col", "row"),
        check_vma=False,
    )
```

```python
import jax
import jax.numpy as jnp
from jax import lax
from jax.experimental import pallas as pl
from jax.experimental.pallas import tpu as pltpu
from jax.sharding import PartitionSpec as P

MESH = pl.DeviceIdType.MESH
F32, BF16 = jnp.float32, jnp.bfloat16
CHUNKS = 8
ROWS, HALF = 128, 64
D, FF = 1536, 3072
PAIR, QUARTER = 768, 384

HIDDEN_SCALE, OUT_SCALE = 2.0**20, 2.0**9

ORDER = (
    ("first", 0), ("pass_on", -1), ("sum_y", 1), ("gather_y", 2), ("second", 3), ("sum_x", 0),
    ("activate", 1), ("gather_x", 2), ("send_out", 3), ("cross", 4),
)
STEPS = CHUNKS + 3


def chunk_at(s, lag):
    t = s - lag
    return t, (t >= 0) & (t < CHUNKS)


def code(v, scale):
    v = v * scale
    return ((v * v) * (v * jnp.abs(v))).astype(BF16)


def decode(coded, scale):
    y = coded.astype(F32)
    r = lax.rsqrt(jnp.maximum(jnp.abs(y), 1e-37))
    return y * (r * r) * (lax.rsqrt(r) * (1.0 / scale))


def kernel(tok_hbm, w1_hbm, bin_ref, w2_hbm, bout_ref, out_ref,
           w1, w2, tok, x1s, x1r, keep1, ys, yr, keepy, x2s, x2r, keep2, hid, po, cr, osend, orecv, acc, y2s, y2r,
           w1_sem, w2_sem, own_sem, tok_ss, tok_rs, fwd_ss, fwd_rs, first_ss, relay_ss,
           x1_ss, x1_rs, y_ss, y_rs, x2_ss, x2_rs, gx_ss, gx_rs, gy_ss, gy_rs, gxx_ss, gxx_rs,
           c_ss, c_rs, o_ss, o_rs, y2_ss, y2_rs):
    row, col = lax.axis_index("row"), lax.axis_index("col")
    x, yh = row // 2, row % 2
    yl, z, core = col // 8, (col // 2) % 4, col % 2
    x_one = x + 1 - 2 * (x % 2)
    x_three = 3 - x
    one = (x_one * 2 + yh, col)
    three = (x_three * 2 + yh, col)
    across = (x * 2 + 1 - yh, col)
    sibling = (row, col + 1 - 2 * core)
    low = (row, (1 - yl) * 8 + z * 2 + core)

    def along_z(d):
        return (row, yl * 8 + ((z + d) % 4) * 2 + core)

    mine = (((x + 1) // 2) % 2, x // 2)
    q = (x // 2, x % 2)
    pair_of = tuple(h * 2 * PAIR + mine[h] * PAIR for h in (0, 1))
    other_pair = tuple(h * 2 * PAIR + (1 - mine[h]) * PAIR for h in (0, 1))
    quarter_of = tuple(pair_of[h] + q[h] * QUARTER for h in (0, 1))
    my_half = pl.ds(pl.multiple_of(yh * HALF, HALF), HALF)
    other_half = pl.ds(pl.multiple_of((1 - yh) * HALF, HALF), HALF)
    dest1, dest2 = (one, three), (three, one)

    def cols(start, size):
        return pl.ds(pl.multiple_of(start, 128), size)

    def remote(src, dst, ss, rs, dev):
        return pltpu.make_async_remote_copy(src_ref=src, dst_ref=dst, send_sem=ss, recv_sem=rs, device_id=dev, device_id_type=MESH)

    w1_order = (other_pair[0], other_pair[1], pair_of[0], pair_of[1])

    def load_w1(i):
        c = cols(w1_order[i], PAIR)
        return pltpu.make_async_copy(w1_hbm.at[:, c], w1.at[:, c], w1_sem.at[i])

    own_rows = pl.ds(pl.multiple_of(core * HALF, HALF), HALF)
    other_rows = pl.ds(pl.multiple_of((1 - core) * HALF, HALF), HALF)
    own = pltpu.make_async_copy(tok_hbm, tok.at[0, own_rows], own_sem)
    own.start()
    for i in range(4):
        load_w1(i).start()
    load_w2 = pltpu.make_async_copy(w2_hbm, w2, w2_sem)
    load_w2.start()

    barrier = pltpu.get_barrier_semaphore()
    partners = [one, three, across, sibling, low] + [along_z(d) for d in (1, 2, 3)]
    for dev in partners:
        pl.semaphore_signal(barrier, inc=1, device_id=dev, device_id_type=MESH)
    pl.semaphore_wait(barrier, len(partners))

    def token_slot(t):
        return tok.at[t, own_rows]

    def to_sibling(t):
        return remote(token_slot(t), token_slot(t), fwd_ss.at[t], fwd_rs.at[t], sibling)

    def from_sibling(t):
        return remote(tok.at[t, other_rows], tok.at[t, other_rows], fwd_ss.at[t], fwd_rs.at[t], sibling)

    own.wait()
    to_sibling(0).start()
    to_low = remote(token_slot(0), token_slot(1), first_ss.at[0], tok_rs.at[1], low)
    to_low.start()
    to_z = []
    for d in (1, 3, 2):
        copy = remote(token_slot(0), token_slot(4 + d), first_ss.at[d], tok_rs.at[4 + d], along_z(4 - d))
        copy.start()
        to_z.append(copy)

    def relay(d):
        return remote(token_slot(1), token_slot(1 + d), relay_ss.at[d - 1], tok_rs.at[1 + d], along_z(4 - d))

    def pass_on(t):
        remote(token_slot(t), token_slot(t), tok_ss.at[0], tok_rs.at[t], low).wait_recv()
        to_sibling(t).start()

        @pl.when(t == 1)
        def _():
            for d in (1, 3, 2):
                relay(d).start()

    def x1_copy(t, h):
        return remote(x1s.at[t % 2, h], x1r.at[t, h], x1_ss.at[t % 2, h], x1_rs.at[t, h], dest1[h])

    def first(t):
        from_sibling(t).wait_recv()
        for i in range(4):
            h = i % 2

            @pl.when(t == 0)
            def _():
                load_w1(i).wait()

            if i < 2:
                @pl.when(t >= 2)
                def _():
                    x1_copy(t, h).wait_send()

            part = jnp.dot(tok[t], w1[:, cols(w1_order[i], PAIR)], preferred_element_type=F32)
            if i < 2:
                x1s[t % 2, h] = code(part, HIDDEN_SCALE)
                x1_copy(t, h).start()
            else:
                keep1[h] = part

    def y_copy(t, h):
        return remote(ys.at[t % 2, h], yr.at[t, h], y_ss.at[t % 2, h], y_rs.at[t, h], across)

    def sum_x(t):
        for h in (0, 1):
            x1_copy(t, h).wait_recv()

            @pl.when(t >= 2)
            def _():
                y_copy(t, h).wait_send()

            ys[t % 2, h] = code(keep1[h, other_half] + decode(x1r[t, h, other_half], HIDDEN_SCALE), HIDDEN_SCALE)
            y_copy(t, h).start()
        for h in (0, 1):
            keepy[h] = keep1[h, my_half] + decode(x1r[t, h, my_half], HIDDEN_SCALE)

    def x2_copy(t, h):
        return remote(x2s.at[t % 2, h], x2r.at[t, h], x2_ss.at[t % 2, h], x2_rs.at[t, h], dest2[h])

    def sum_y(t):
        for h in (0, 1):
            y_copy(t, h).wait_recv()

            @pl.when(t >= 2)
            def _():
                x2_copy(t, h).wait_send()

            gone = cols((1 - q[h]) * QUARTER, QUARTER)
            x2s[t % 2, h] = code(keepy[h, :, gone] + decode(yr[t, h, :, gone], HIDDEN_SCALE), HIDDEN_SCALE)
            x2_copy(t, h).start()
        for h in (0, 1):
            kept = cols(q[h] * QUARTER, QUARTER)
            keep2[h] = keepy[h, :, kept] + decode(yr[t, h, :, kept], HIDDEN_SCALE)

    def hid_copy(t, rows, start, size, ss, rs, dev):
        c = cols(start, size)
        return remote(hid.at[t, rows, c], hid.at[t, rows, c], ss, rs, dev)

    def gx_copy(t, h):
        return hid_copy(t, my_half, quarter_of[h], QUARTER, gx_ss.at[t, h], gx_rs.at[t, h], dest2[h])

    def gy_copy(t, h):
        return hid_copy(t, my_half, pair_of[h], PAIR, gy_ss.at[t, h], gy_rs.at[t, h], across)

    def gxx_copy(t, h):
        return hid_copy(t, pl.ds(0, ROWS), pair_of[h], PAIR, gxx_ss.at[t, h], gxx_rs.at[t, h], dest1[h])

    def activate(t):
        for h in (0, 1):
            x2_copy(t, h).wait_recv()
            c = cols(quarter_of[h], QUARTER)
            summed = keep2[h] + decode(x2r[t, h], HIDDEN_SCALE)
            hid[t, my_half, c] = jax.nn.gelu(summed + bin_ref[:, c], approximate=True).astype(BF16)
            gx_copy(t, h).start()

    def gather_y(t):
        for h in (0, 1):
            gx_copy(t, h).wait_recv()
            gy_copy(t, h).start()

    def gather_x(t):
        for h in (0, 1):
            gy_copy(t, h).wait_recv()
            gxx_copy(t, h).start()

    def c_copy(t):
        return remote(po.at[t % 2, other_rows], cr.at[t], c_ss.at[t % 2], c_rs.at[t], sibling)

    def second(t):
        @pl.when(t == 0)
        def _():
            load_w2.wait()

        @pl.when(t >= 2)
        def _():
            c_copy(t).wait_send()

        for h in (0, 1):
            gxx_copy(t, h).wait_recv()
        for i in range(2):
            c = pl.ds(i * PAIR, PAIR)
            po[t % 2, :, c] = jnp.dot(hid[t], w2[:, c], preferred_element_type=F32)
        c_copy(t).start()

    def o_copy(t):
        far = (t + 3) // 4 % 2
        return remote(osend.at[t % 2], orecv.at[t], o_ss.at[t % 2], o_rs.at[t], along_z((t + 3 * far) % 4))

    def send_out(t):
        c_copy(t).wait_recv()

        @pl.when(t < 2)
        def _():
            acc[t] = po[t % 2, own_rows] + cr[t]

        @pl.when(t >= 2)
        def _():
            @pl.when(t >= 4)
            def _():
                o_copy(t).wait_send()

            osend[t % 2] = code(po[t % 2, own_rows] + cr[t], OUT_SCALE)
            o_copy(t).start()

    y2_copy = remote(y2s, y2r, y2_ss, y2_rs, low)

    def cross(t):
        @pl.when(t == 4)
        def _():
            for i in (2, 3, 4):
                o_copy(i).wait_recv()
            y2s[...] = code(acc[1] + sum(decode(orecv[i], OUT_SCALE) for i in (2, 3, 4)), OUT_SCALE)
            y2_copy.start()

    tasks = dict(first=first, pass_on=pass_on, sum_x=sum_x, sum_y=sum_y, activate=activate, gather_y=gather_y,
                 gather_x=gather_x, second=second, send_out=send_out, cross=cross)

    def step(s, _):
        for name, *at in ORDER:
            t, runs = chunk_at(s, *at)

            @pl.when(runs & (t >= (1 if name == "pass_on" else 0)))
            def _():
                tasks[name](t)

        return 0

    lax.fori_loop(0, STEPS, step, 0)

    for i in (5, 6, 7):
        o_copy(i).wait_recv()
    y2_copy.wait_recv()
    far = sum(decode(orecv[i], OUT_SCALE) for i in (5, 6, 7))
    out_ref[...] = acc[0] + far + decode(y2r[...], OUT_SCALE) + bout_ref[...]

    to_low.wait_send()
    for copy in to_z:
        copy.wait_send()
    for d in (1, 2, 3):
        relay(d).wait_send()
    for t in range(CHUNKS):
        to_sibling(t).wait_send()
        for h in (0, 1):
            gx_copy(t, h).wait_send()
            gy_copy(t, h).wait_send()
            gxx_copy(t, h).wait_send()
    for t in (CHUNKS - 2, CHUNKS - 1):
        for h in (0, 1):
            x1_copy(t, h).wait_send()
            x2_copy(t, h).wait_send()
            y_copy(t, h).wait_send()
        c_copy(t).wait_send()
        o_copy(t).wait_send()
    y2_copy.wait_send()


def per_device(tokens, w_in, b_in, w_out, b_out):
    any_space, vmem = pl.BlockSpec(memory_space=pl.ANY), pl.BlockSpec(memory_space=pltpu.VMEM)
    dma = pltpu.SemaphoreType.DMA
    n = CHUNKS
    scratch = [
        pltpu.VMEM((D, FF), BF16), pltpu.VMEM((FF, D), BF16), pltpu.VMEM((n, ROWS, D), BF16),
        pltpu.VMEM((2, 2, ROWS, PAIR), BF16), pltpu.VMEM((n, 2, ROWS, PAIR), BF16), pltpu.VMEM((2, ROWS, PAIR), F32),
        pltpu.VMEM((2, 2, HALF, PAIR), BF16), pltpu.VMEM((n, 2, HALF, PAIR), BF16), pltpu.VMEM((2, HALF, PAIR), F32),
        pltpu.VMEM((2, 2, HALF, QUARTER), BF16), pltpu.VMEM((n, 2, HALF, QUARTER), BF16), pltpu.VMEM((2, HALF, QUARTER), F32),
        pltpu.VMEM((n, ROWS, FF), BF16), pltpu.VMEM((2, ROWS, D), F32), pltpu.VMEM((n, HALF, D), F32),
        pltpu.VMEM((2, HALF, D), BF16), pltpu.VMEM((n, HALF, D), BF16), pltpu.VMEM((2, HALF, D), F32),
        pltpu.VMEM((HALF, D), BF16), pltpu.VMEM((HALF, D), BF16),
        dma((4,)), dma, dma, dma((1,)), dma((n,)), dma((n,)), dma((n,)), dma((4,)), dma((3,)),
        dma((2, 2)), dma((n, 2)), dma((2, 2)), dma((n, 2)), dma((2, 2)), dma((n, 2)),
        dma((n, 2)), dma((n, 2)), dma((n, 2)), dma((n, 2)), dma((n, 2)), dma((n, 2)),
        dma((2,)), dma((n,)), dma((2,)), dma((n,)), dma, dma,
    ]
    return pl.pallas_call(
        kernel,
        out_shape=jax.ShapeDtypeStruct((HALF, D), F32),
        in_specs=[any_space, any_space, vmem, any_space, vmem],
        out_specs=vmem,
        scratch_shapes=scratch,
        compiler_params=pltpu.CompilerParams(collective_id=0, has_side_effects=True, vmem_limit_bytes=60 * 2**20),
        cost_estimate=pl.CostEstimate(flops=4 * 1024 * D * FF, bytes_accessed=4 * D * FF, transcendentals=1024 * QUARTER),
    )(tokens, w_in, b_in.astype(F32).reshape(1, FF), w_out, b_out.astype(F32).reshape(1, D))


def solution(mesh):
    return jax.shard_map(
        per_device,
        mesh=mesh,
        in_specs=(P("col", "row"), P("row", "col"), P("col"), P("col", "row"), P("row")),
        out_specs=P("col", "row"),
        check_vma=False,
    )
```

```python
import jax
import jax.numpy as jnp
from jax import lax
from jax.experimental import pallas as pl
from jax.experimental.pallas import tpu as pltpu
from jax.sharding import PartitionSpec as P

MESH = pl.DeviceIdType.MESH
F32, BF16 = jnp.float32, jnp.bfloat16
GROUPS, SLOTS = 8, 16
ROWS, SLOT, HALF = 128, 64, 32
D, FF = 1536, 3072
PAIR, QUARTER = 768, 384

HIDDEN_SCALE, OUT_SCALE = 2.0**20, 2.0**9

ORDER = (
    ("sum_y0", 3), ("gather_x1", 7), ("first", 0), ("second", 9), ("sum_x1", 2), ("send_out", 10), ("pass_on", -1),
    ("activate1", 4), ("gather_y1", 5), ("sum_y1", 3), ("sum_x0", 1), ("gather_x0", 6), ("gather_y0", 4), ("cross", 12),
    ("activate0", 3),
)
STEPS = 18


def code(v, scale):
    v = v * scale
    return ((v * v) * (v * jnp.abs(v))).astype(BF16)


def decode(coded, scale):
    y = coded.astype(F32)
    r = lax.rsqrt(jnp.maximum(jnp.abs(y), 1e-37))
    return y * (r * r) * (lax.rsqrt(r) * (1.0 / scale))


def kernel(tok_hbm, w1_hbm, bin_ref, w2_hbm, bout_ref, out_ref,
           w1, w2, tok, x1s, x1r, keep, ys, yr, x2s, x2r, hid, po, cr, osend, orecv, acc, y2s, y2r,
           w1_sem, w2_sem, own_sem, first_ss, tok_rs, relay_ss, fwd_ss, fwd_rs,
           x1_ss, x1_rs, y_ss, y_rs, x2_ss, x2_rs, gx_ss, gx_rs, gy_ss, gy_rs, gxx_ss, gxx_rs,
           c_ss, c_rs, o_ss, o_rs, y2_ss, y2_rs):
    row, col = lax.axis_index("row"), lax.axis_index("col")
    x, yh = row // 2, row % 2
    yl, z, core = col // 8, (col // 2) % 4, col % 2
    x_one = x + 1 - 2 * (x % 2)
    x_three = 3 - x
    one = (x_one * 2 + yh, col)
    three = (x_three * 2 + yh, col)
    across = (x * 2 + 1 - yh, col)
    sibling = (row, col + 1 - 2 * core)
    low = (row, (1 - yl) * 8 + z * 2 + core)

    def along_z(d):
        return (row, yl * 8 + ((z + d) % 4) * 2 + core)

    def cols(start, size):
        return pl.ds(pl.multiple_of(start, 128), size)

    def rows(start, size=HALF):
        return pl.ds(pl.multiple_of(start, HALF), size)

    mine = (((x + 1) // 2) % 2, x // 2)
    q = (x // 2, x % 2)
    pair_of = tuple(h * 2 * PAIR + mine[h] * PAIR for h in (0, 1))
    other_pair = tuple(h * 2 * PAIR + (1 - mine[h]) * PAIR for h in (0, 1))
    quarter_of = tuple(pair_of[h] + q[h] * QUARTER for h in (0, 1))
    kept = tuple(cols(q[h] * QUARTER, QUARTER) for h in (0, 1))
    gone = tuple(cols((1 - q[h]) * QUARTER, QUARTER) for h in (0, 1))
    dest1, dest2 = (one, three), (three, one)
    my_half, other_half = rows(yh * HALF), rows((1 - yh) * HALF)
    own_rows, other_rows = rows(core * HALF), rows((1 - core) * HALF)

    def remote(src, dst, ss, rs, dev):
        return pltpu.make_async_remote_copy(src_ref=src, dst_ref=dst, send_sem=ss, recv_sem=rs, device_id=dev, device_id_type=MESH)

    w1_order = (other_pair[0], other_pair[1], pair_of[0], pair_of[1])

    def load_w1(i):
        c = cols(w1_order[i], PAIR)
        return pltpu.make_async_copy(w1_hbm.at[:, c], w1.at[:, c], w1_sem.at[i])

    own = pltpu.make_async_copy(tok_hbm, tok.at[0, :, own_rows], own_sem)
    own.start()
    for i in range(4):
        load_w1(i).start()
    load_w2 = pltpu.make_async_copy(w2_hbm, w2, w2_sem)
    load_w2.start()

    barrier = pltpu.get_barrier_semaphore()
    partners = [one, three, across, sibling, low] + [along_z(d) for d in (1, 2, 3)]
    for dev in partners:
        pl.semaphore_signal(barrier, inc=1, device_id=dev, device_id_type=MESH)
    pl.semaphore_wait(barrier, len(partners))

    def block(r):
        return tok.at[r, :, own_rows]

    def to_sibling(r):
        return remote(block(r), block(r), fwd_ss.at[r], fwd_rs.at[r], sibling)

    def from_sibling(r):
        return remote(tok.at[r, :, other_rows], tok.at[r, :, other_rows], fwd_ss.at[r], fwd_rs.at[r], sibling)

    own.wait()
    to_sibling(0).start()
    to_low = remote(block(0), block(1), first_ss.at[0], tok_rs.at[1], low)
    to_low.start()

    def to_z(d):
        return remote(block(0), block(4 + d), first_ss.at[d], tok_rs.at[4 + d], along_z(4 - d))

    for d in (1, 3, 2):
        to_z(d).start()

    def relay(d):
        return remote(block(1), block(1 + d), relay_ss.at[d - 1], tok_rs.at[1 + d], along_z(4 - d))

    def pass_on(r):
        @pl.when(r >= 1)
        def _():
            remote(block(r), block(r), fwd_ss.at[r], tok_rs.at[r], low).wait_recv()
            to_sibling(r).start()

        @pl.when(r == 1)
        def _():
            for d in (1, 3, 2):
                relay(d).start()

    def x1_copy(k, h):
        return remote(x1s.at[k, h], x1r.at[k, h], x1_ss.at[k, h], x1_rs.at[k, h], dest1[h])

    def first(r):
        from_sibling(r).wait_recv()
        tokens = tok[r].reshape(ROWS, D)
        for i in range(4):
            h = i % 2

            @pl.when(r == 0)
            def _():
                load_w1(i).wait()

            part = jnp.dot(tokens, w1[:, cols(w1_order[i], PAIR)], preferred_element_type=F32)
            for u in (0, 1):
                if i < 2:
                    x1s[2 * r + u, h] = code(part[u * SLOT : (u + 1) * SLOT], HIDDEN_SCALE)
                    x1_copy(2 * r + u, h).start()
                else:
                    keep[2 * r + u, h] = part[u * SLOT : (u + 1) * SLOT]

    def y_copy(k, h):
        return remote(ys.at[k, h], yr.at[k, h], y_ss.at[k, h], y_rs.at[k, h], across)

    def sum_x(k):
        for h in (0, 1):
            x1_copy(k, h).wait_recv()
            ys[k, h] = code(keep[k, h, other_half] + decode(x1r[k, h, other_half], HIDDEN_SCALE), HIDDEN_SCALE)
            y_copy(k, h).start()
        for h in (0, 1):
            keep[k, h, my_half] += decode(x1r[k, h, my_half], HIDDEN_SCALE)

    def x2_copy(k, h):
        return remote(x2s.at[k, h], x2r.at[k, h], x2_ss.at[k, h], x2_rs.at[k, h], dest2[h])

    def sum_y(k):
        for h in (0, 1):
            y_copy(k, h).wait_recv()
            x2s[k, h] = code(keep[k, h, my_half, gone[h]] + decode(yr[k, h, :, gone[h]], HIDDEN_SCALE), HIDDEN_SCALE)
            x2_copy(k, h).start()
        for h in (0, 1):
            keep[k, h, my_half, kept[h]] += decode(yr[k, h, :, kept[h]], HIDDEN_SCALE)

    def hid_copy(k, which, start, size, ss, rs, dev):
        c = cols(start, size)
        return remote(hid.at[k, which, c], hid.at[k, which, c], ss, rs, dev)

    def gx_copy(k, h):
        return hid_copy(k, my_half, quarter_of[h], QUARTER, gx_ss.at[k, h], gx_rs.at[k, h], dest2[h])

    def gy_copy(k, h):
        return hid_copy(k, my_half, pair_of[h], PAIR, gy_ss.at[k, h], gy_rs.at[k, h], across)

    def gxx_copy(k, h):
        return hid_copy(k, pl.ds(0, SLOT), pair_of[h], PAIR, gxx_ss.at[k, h], gxx_rs.at[k, h], dest1[h])

    def activate(k):
        for h in (0, 1):
            x2_copy(k, h).wait_recv()
            c = cols(quarter_of[h], QUARTER)
            summed = keep[k, h, my_half, kept[h]] + decode(x2r[k, h], HIDDEN_SCALE)
            hid[k, my_half, c] = jax.nn.gelu(summed + bin_ref[:, c], approximate=True).astype(BF16)
            gx_copy(k, h).start()

    def gather_y(k):
        for h in (0, 1):
            gx_copy(k, h).wait_recv()
            gy_copy(k, h).start()

    def gather_x(k):
        for h in (0, 1):
            gy_copy(k, h).wait_recv()
            gxx_copy(k, h).start()
        for h in (0, 1):
            x1_copy(k, h).wait_send()
            y_copy(k, h).wait_send()
            x2_copy(k, h).wait_send()

    def c_copy(m):
        r = (m + 1) % GROUPS
        return remote(po.at[m % 2, :, other_rows], cr.at[r], c_ss.at[m % 2], c_rs.at[r], sibling)

    def second(m):
        r = (m + 1) % GROUPS

        @pl.when(m == 0)
        def _():
            load_w2.wait()

        @pl.when(m >= 2)
        def _():
            c_copy(m - 2).wait_send()

        for u in (0, 1):
            for h in (0, 1):
                gxx_copy(2 * r + u, h).wait_recv()
        hidden = hid[pl.ds(2 * r, 2)].reshape(ROWS, FF)
        for i in range(2):
            c = pl.ds(i * PAIR, PAIR)
            po[m % 2, :, :, c] = jnp.dot(hidden, w2[:, c], preferred_element_type=F32).reshape(2, SLOT, PAIR)
        c_copy(m).start()
        for u in (0, 1):
            for h in (0, 1):
                gx_copy(2 * r + u, h).wait_send()
                gy_copy(2 * r + u, h).wait_send()

    def o_copy(m):
        r = (m + 1) % GROUPS
        far = (r + 3) // 4 % 2
        return remote(osend.at[m % 2], orecv.at[r], o_ss.at[m % 2], o_rs.at[r], along_z((r + 3 * far) % 4))

    def send_out(m):
        r = (m + 1) % GROUPS
        c_copy(m).wait_recv()

        @pl.when(r < 2)
        def _():
            acc[r] = po[m % 2, :, own_rows] + cr[r]

        @pl.when(r >= 2)
        def _():
            @pl.when(m >= 3)
            def _():
                o_copy(m - 2).wait_send()

            osend[m % 2] = code(po[m % 2, :, own_rows] + cr[r], OUT_SCALE)
            o_copy(m).start()

        to_sibling(r).wait_send()
        for u in (0, 1):
            for h in (0, 1):
                gxx_copy(2 * r + u, h).wait_send()

    y2_copy = remote(y2s, y2r, y2_ss, y2_rs, low)

    def cross(m):
        @pl.when(m == 3)
        def _():
            for r in (2, 3, 4):
                o_copy(r - 1).wait_recv()
            y2s[...] = code(acc[1] + sum(decode(orecv[r], OUT_SCALE) for r in (2, 3, 4)), OUT_SCALE)
            y2_copy.start()
            to_low.wait_send()
            for d in (1, 2, 3):
                to_z(d).wait_send()
                relay(d).wait_send()

    tasks = dict(first=first, pass_on=pass_on, sum_x=sum_x, sum_y=sum_y, activate=activate, gather_y=gather_y,
                 gather_x=gather_x, second=second, send_out=send_out, cross=cross)

    def step(s, _):
        for name, lag in ORDER:
            p = s - lag

            @pl.when((p >= 0) & (p < GROUPS))
            def _():
                if name[-1] in "01":
                    tasks[name[:-1]]((2 * p + int(name[-1]) + 1) % SLOTS)
                else:
                    tasks[name](p)

        return 0

    lax.fori_loop(0, STEPS, step, 0)

    for r in (5, 6, 7):
        o_copy(r - 1).wait_recv()
    y2_copy.wait_recv()
    far = sum(decode(orecv[r], OUT_SCALE) for r in (5, 6, 7))
    out_ref[...] = acc[0] + far + decode(y2r[...], OUT_SCALE) + bout_ref[...]

    for m in (GROUPS - 2, GROUPS - 1):
        c_copy(m).wait_send()
    for m in (GROUPS - 3, GROUPS - 2):
        o_copy(m).wait_send()
    y2_copy.wait_send()


def per_device(tokens, w_in, b_in, w_out, b_out):
    any_space, vmem = pl.BlockSpec(memory_space=pl.ANY), pl.BlockSpec(memory_space=pltpu.VMEM)
    dma = pltpu.SemaphoreType.DMA
    g, n = GROUPS, SLOTS
    scratch = [
        pltpu.VMEM((D, FF), BF16), pltpu.VMEM((FF, D), BF16), pltpu.VMEM((g, 2, SLOT, D), BF16),
        pltpu.VMEM((n, 2, SLOT, PAIR), BF16), pltpu.VMEM((n, 2, SLOT, PAIR), BF16), pltpu.VMEM((n, 2, SLOT, PAIR), F32),
        pltpu.VMEM((n, 2, HALF, PAIR), BF16), pltpu.VMEM((n, 2, HALF, PAIR), BF16),
        pltpu.VMEM((n, 2, HALF, QUARTER), BF16), pltpu.VMEM((n, 2, HALF, QUARTER), BF16),
        pltpu.VMEM((n, SLOT, FF), BF16), pltpu.VMEM((2, 2, SLOT, D), F32), pltpu.VMEM((g, 2, HALF, D), F32),
        pltpu.VMEM((2, 2, HALF, D), BF16), pltpu.VMEM((g, 2, HALF, D), BF16), pltpu.VMEM((2, 2, HALF, D), F32),
        pltpu.VMEM((2, HALF, D), BF16), pltpu.VMEM((2, HALF, D), BF16),
        dma((4,)), dma, dma, dma((4,)), dma((g,)), dma((3,)), dma((g,)), dma((g,)),
        dma((n, 2)), dma((n, 2)), dma((n, 2)), dma((n, 2)), dma((n, 2)), dma((n, 2)),
        dma((n, 2)), dma((n, 2)), dma((n, 2)), dma((n, 2)), dma((n, 2)), dma((n, 2)),
        dma((2,)), dma((g,)), dma((2,)), dma((g,)), dma, dma,
    ]
    out = pl.pallas_call(
        kernel,
        out_shape=jax.ShapeDtypeStruct((2, HALF, D), F32),
        in_specs=[any_space, any_space, vmem, any_space, vmem],
        out_specs=vmem,
        scratch_shapes=scratch,
        compiler_params=pltpu.CompilerParams(collective_id=0, has_side_effects=True, vmem_limit_bytes=62 * 2**20),
        cost_estimate=pl.CostEstimate(flops=4 * 1024 * D * FF, bytes_accessed=4 * D * FF, transcendentals=1024 * QUARTER),
    )(tokens.reshape(2, HALF, D), w_in, b_in.astype(F32).reshape(1, FF), w_out, b_out.astype(F32).reshape(1, D))
    return out.reshape(2 * HALF, D)


def solution(mesh):
    return jax.shard_map(
        per_device,
        mesh=mesh,
        in_specs=(P("col", "row"), P("row", "col"), P("col"), P("col", "row"), P("row")),
        out_specs=P("col", "row"),
        check_vma=False,
    )
```

```python
import jax
import jax.numpy as jnp
from jax import lax
from jax.experimental import pallas as pl
from jax.experimental.pallas import tpu as pltpu
from jax.sharding import PartitionSpec as P

MESH = pl.DeviceIdType.MESH
F32, BF16 = jnp.float32, jnp.bfloat16
GROUPS, SLOTS = 8, 16
ROWS, SLOT, HALF = 128, 64, 32
D, FF = 1536, 3072
PAIR, QUARTER = 768, 384

HIDDEN_SCALE, OUT_SCALE = 2.0**20, 2.0**9

ORDER = (
    ("first", 0), ("sum_x1", 1), ("gather_y0", 5), ("second", 9), ("activate1", 3), ("sum_y1", 2), ("activate0", 2),
    ("gather_x1", 7), ("cross", 11), ("sum_y0", 1), ("sum_x0", 0), ("pass_on", -1), ("send_out", 9), ("gather_x0", 6),
    ("gather_y1", 5),
)
STEPS = 17


def code(v, scale):
    v = v * scale
    return ((v * v) * (v * jnp.abs(v))).astype(BF16)


def decode(coded, scale):
    y = coded.astype(F32)
    r = lax.rsqrt(jnp.maximum(jnp.abs(y), 1e-37))
    return y * (r * r) * (lax.rsqrt(r) * (1.0 / scale))


def kernel(tok_hbm, w1_hbm, bin_ref, w2_hbm, out_ref,
           w1, w2, bias, tok, x1s, x1r, keep, ys, yr, x2s, x2r, hid, po, cr, osend, orecv, acc, y2s, y2r,
           w1_sem, w2_sem, own_sem, first_ss, tok_rs, relay_ss, fwd_ss, fwd_rs,
           x1_ss, x1_rs, y_ss, y_rs, x2_ss, x2_rs, gx_ss, gx_rs, gy_ss, gy_rs, gxx_ss, gxx_rs,
           c_ss, c_rs, o_ss, o_rs, y2_ss, y2_rs):
    row, col = lax.axis_index("row"), lax.axis_index("col")
    x, yh = row // 2, row % 2
    yl, z, core = col // 8, (col // 2) % 4, col % 2
    x_one = x + 1 - 2 * (x % 2)
    x_three = 3 - x
    one = (x_one * 2 + yh, col)
    three = (x_three * 2 + yh, col)
    across = (x * 2 + 1 - yh, col)
    sibling = (row, col + 1 - 2 * core)
    low = (row, (1 - yl) * 8 + z * 2 + core)

    def along_z(d):
        return (row, yl * 8 + ((z + d) % 4) * 2 + core)

    def cols(start, size):
        return pl.ds(pl.multiple_of(start, 128), size)

    def rows(start, size=HALF):
        return pl.ds(pl.multiple_of(start, HALF), size)

    mine = (((x + 1) // 2) % 2, x // 2)
    q = (x // 2, x % 2)
    pair_of = tuple(h * 2 * PAIR + mine[h] * PAIR for h in (0, 1))
    other_pair = tuple(h * 2 * PAIR + (1 - mine[h]) * PAIR for h in (0, 1))
    quarter_of = tuple(pair_of[h] + q[h] * QUARTER for h in (0, 1))
    kept = tuple(cols(q[h] * QUARTER, QUARTER) for h in (0, 1))
    gone = tuple(cols((1 - q[h]) * QUARTER, QUARTER) for h in (0, 1))
    dest1, dest2 = (one, three), (three, one)
    my_half, other_half = rows(yh * HALF), rows((1 - yh) * HALF)
    own_rows, other_rows = rows(core * HALF), rows((1 - core) * HALF)

    def remote(src, dst, ss, rs, dev):
        return pltpu.make_async_remote_copy(src_ref=src, dst_ref=dst, send_sem=ss, recv_sem=rs, device_id=dev, device_id_type=MESH)

    w1_order = (other_pair[0], other_pair[1], pair_of[0], pair_of[1])

    def load_w1(i):
        c = cols(w1_order[i], PAIR)
        return pltpu.make_async_copy(w1_hbm.at[:, c], w1.at[:, c], w1_sem.at[i])

    own = pltpu.make_async_copy(tok_hbm, tok.at[0, :, own_rows], own_sem)
    own.start()
    for i in range(4):
        load_w1(i).start()
    load_w2 = pltpu.make_async_copy(w2_hbm, w2, w2_sem)

    bias[...] = bin_ref[...].astype(F32).reshape(1, FF)
    barrier = pltpu.get_barrier_semaphore()
    partners = [one, three, across, sibling, low] + [along_z(d) for d in (1, 2, 3)]
    for dev in partners:
        pl.semaphore_signal(barrier, inc=1, device_id=dev, device_id_type=MESH)
    pl.semaphore_wait(barrier, len(partners))

    near = {1: 1, 2: 6, 3: 7}

    def block(r):
        return tok.at[r, :, own_rows]

    def to_sibling(r):
        return remote(block(r), block(r), fwd_ss.at[r], fwd_rs.at[r], sibling)

    def from_sibling(r):
        return remote(tok.at[r, :, other_rows], tok.at[r, :, other_rows], fwd_ss.at[r], fwd_rs.at[r], sibling)

    own.wait()
    to_sibling(0).start()
    to_low = remote(block(0), block(2), first_ss.at[0], tok_rs.at[2], low)
    to_low.start()

    def to_z(d):
        return remote(block(0), block(near[d]), first_ss.at[d], tok_rs.at[near[d]], along_z(4 - d))

    to_z(1).start()

    def relay(d):
        return remote(block(2), block(2 + d), relay_ss.at[d - 1], tok_rs.at[2 + d], along_z(4 - d))

    def take(r):
        remote(block(r), block(r), fwd_ss.at[r], tok_rs.at[r], low).wait_recv()
        to_sibling(r).start()

    def pass_on(p):
        @pl.when(p == 1)
        def _():
            take(1)
            take(2)
            for d in (1, 3, 2):
                relay(d).start()
            for d in (3, 2):
                to_z(d).start()

        @pl.when((p > 1) & (p < GROUPS - 1))
        def _():
            take(p + 1)

    def x1_copy(k, h):
        return remote(x1s.at[k, h], x1r.at[k, h], x1_ss.at[k, h], x1_rs.at[k, h], dest1[h])

    def first(r):
        from_sibling(r).wait_recv()
        tokens = tok[r].reshape(ROWS, D)

        @pl.when(r == 1)
        def _():
            load_w2.start()

        for i in range(4):
            h = i % 2

            @pl.when(r == 0)
            def _():
                load_w1(i).wait()

            part = jnp.dot(tokens, w1[:, cols(w1_order[i], PAIR)], preferred_element_type=F32)
            for u in (0, 1):
                if i < 2:
                    x1s[2 * r + u, h] = code(part[u * SLOT : (u + 1) * SLOT], HIDDEN_SCALE)
                    x1_copy(2 * r + u, h).start()
                else:
                    keep[2 * r + u, h] = part[u * SLOT : (u + 1) * SLOT]

    def y_copy(k, h):
        return remote(ys.at[k, h], yr.at[k, h], y_ss.at[k, h], y_rs.at[k, h], across)

    def sum_x(k):
        for h in (0, 1):
            x1_copy(k, h).wait_recv()
            ys[k, h] = code(keep[k, h, other_half] + decode(x1r[k, h, other_half], HIDDEN_SCALE), HIDDEN_SCALE)
            y_copy(k, h).start()
        for h in (0, 1):
            keep[k, h, my_half] += decode(x1r[k, h, my_half], HIDDEN_SCALE)

    def x2_copy(k, h):
        return remote(x2s.at[k, h], x2r.at[k, h], x2_ss.at[k, h], x2_rs.at[k, h], dest2[h])

    def sum_y(k):
        for h in (0, 1):
            y_copy(k, h).wait_recv()
            x2s[k, h] = code(keep[k, h, my_half, gone[h]] + decode(yr[k, h, :, gone[h]], HIDDEN_SCALE), HIDDEN_SCALE)
            x2_copy(k, h).start()
        for h in (0, 1):
            keep[k, h, my_half, kept[h]] += decode(yr[k, h, :, kept[h]], HIDDEN_SCALE)

    def hid_copy(k, which, start, size, ss, rs, dev):
        c = cols(start, size)
        return remote(hid.at[k, which, c], hid.at[k, which, c], ss, rs, dev)

    def gx_copy(k, h):
        return hid_copy(k, my_half, quarter_of[h], QUARTER, gx_ss.at[k, h], gx_rs.at[k, h], dest2[h])

    def gy_copy(k, h):
        return hid_copy(k, my_half, pair_of[h], PAIR, gy_ss.at[k, h], gy_rs.at[k, h], across)

    def gxx_copy(k, h):
        return hid_copy(k, pl.ds(0, SLOT), pair_of[h], PAIR, gxx_ss.at[k, h], gxx_rs.at[k, h], dest1[h])

    def activate(k):
        for h in (0, 1):
            x2_copy(k, h).wait_recv()
            c = cols(quarter_of[h], QUARTER)
            summed = keep[k, h, my_half, kept[h]] + decode(x2r[k, h], HIDDEN_SCALE)
            hid[k, my_half, c] = jax.nn.gelu(summed + bias[:, c], approximate=True).astype(BF16)
            gx_copy(k, h).start()

    def gather_y(k):
        for h in (0, 1):
            gx_copy(k, h).wait_recv()
            gy_copy(k, h).start()

    def gather_x(k):
        for h in (0, 1):
            gy_copy(k, h).wait_recv()
            gxx_copy(k, h).start()
        for h in (0, 1):
            x1_copy(k, h).wait_send()
            y_copy(k, h).wait_send()
            x2_copy(k, h).wait_send()

    def c_copy(m):
        r = (m + 1) % GROUPS
        return remote(po.at[m % 2, :, other_rows], cr.at[r], c_ss.at[m % 2], c_rs.at[r], sibling)

    def second(m):
        r = (m + 1) % GROUPS

        @pl.when(m == 0)
        def _():
            load_w2.wait()

        @pl.when(m >= 2)
        def _():
            c_copy(m - 2).wait_send()

        for u in (0, 1):
            for h in (0, 1):
                gxx_copy(2 * r + u, h).wait_recv()
        hidden = hid[pl.ds(2 * r, 2)].reshape(ROWS, FF)
        for i in range(2):
            c = pl.ds(i * PAIR, PAIR)
            po[m % 2, :, :, c] = jnp.dot(hidden, w2[:, c], preferred_element_type=F32).reshape(2, SLOT, PAIR)
        c_copy(m).start()
        for u in (0, 1):
            for h in (0, 1):
                gx_copy(2 * r + u, h).wait_send()
                gy_copy(2 * r + u, h).wait_send()

    def o_copy(m):
        r = (m + 1) % GROUPS
        far = (r + 2) // 4 % 2
        return remote(osend.at[m % 2], orecv.at[r], o_ss.at[m % 2], o_rs.at[r], along_z((r + 2 * far) % 4))

    def send_out(m):
        r = (m + 1) % GROUPS
        c_copy(m).wait_recv()

        @pl.when((m == 1) | (m == 7))
        def _():
            acc[m // 4] = po[m % 2, :, own_rows] + cr[r]

        @pl.when((m != 1) & (m != 7))
        def _():
            @pl.when(m == 2)
            def _():
                o_copy(0).wait_send()

            @pl.when(m >= 4)
            def _():
                o_copy(m - 2).wait_send()

            osend[m % 2] = code(po[m % 2, :, own_rows] + cr[r], OUT_SCALE)
            o_copy(m).start()

        to_sibling(r).wait_send()
        for u in (0, 1):
            for h in (0, 1):
                gxx_copy(2 * r + u, h).wait_send()

    y2_copy = remote(y2s, y2r, y2_ss, y2_rs, low)

    def cross(m):
        @pl.when(m == 4)
        def _():
            for r in (3, 4, 5):
                o_copy(r - 1).wait_recv()
            y2s[...] = code(acc[0] + sum(decode(orecv[r], OUT_SCALE) for r in (3, 4, 5)), OUT_SCALE)
            y2_copy.start()
            to_low.wait_send()
            for d in (1, 2, 3):
                to_z(d).wait_send()
                relay(d).wait_send()

    tasks = dict(first=first, pass_on=pass_on, sum_x=sum_x, sum_y=sum_y, activate=activate, gather_y=gather_y,
                 gather_x=gather_x, second=second, send_out=send_out, cross=cross)

    def step(s, _):
        for name, lag in ORDER:
            p = s - lag

            @pl.when((p >= 0) & (p < GROUPS))
            def _():
                if name[-1] in "01":
                    r = (p + 1) % GROUPS if name.startswith("gather") else p
                    tasks[name[:-1]](2 * r + int(name[-1]))
                else:
                    tasks[name](p)

        return 0

    lax.fori_loop(0, STEPS, step, 0)

    for r in (1, 6, 7):
        o_copy(r - 1).wait_recv()
    y2_copy.wait_recv()
    far = sum(decode(orecv[r], OUT_SCALE) for r in (1, 6, 7))
    out_ref[...] = acc[1] + far + decode(y2r[...], OUT_SCALE)

    for m in (GROUPS - 2, GROUPS - 1):
        c_copy(m).wait_send()
    for m in (5, 6):
        o_copy(m).wait_send()
    y2_copy.wait_send()


def per_device(tokens, w_in, b_in, w_out, b_out):
    any_space, vmem = pl.BlockSpec(memory_space=pl.ANY), pl.BlockSpec(memory_space=pltpu.VMEM)
    dma = pltpu.SemaphoreType.DMA
    g, n = GROUPS, SLOTS
    scratch = [
        pltpu.VMEM((D, FF), BF16), pltpu.VMEM((FF, D), BF16), pltpu.VMEM((1, FF), F32), pltpu.VMEM((g, 2, SLOT, D), BF16),
        pltpu.VMEM((n, 2, SLOT, PAIR), BF16), pltpu.VMEM((n, 2, SLOT, PAIR), BF16), pltpu.VMEM((n, 2, SLOT, PAIR), F32),
        pltpu.VMEM((n, 2, HALF, PAIR), BF16), pltpu.VMEM((n, 2, HALF, PAIR), BF16),
        pltpu.VMEM((n, 2, HALF, QUARTER), BF16), pltpu.VMEM((n, 2, HALF, QUARTER), BF16),
        pltpu.VMEM((n, SLOT, FF), BF16), pltpu.VMEM((2, 2, SLOT, D), F32), pltpu.VMEM((g, 2, HALF, D), F32),
        pltpu.VMEM((2, 2, HALF, D), BF16), pltpu.VMEM((g, 2, HALF, D), BF16), pltpu.VMEM((2, 2, HALF, D), F32),
        pltpu.VMEM((2, HALF, D), BF16), pltpu.VMEM((2, HALF, D), BF16),
        dma((4,)), dma, dma, dma((4,)), dma((g,)), dma((3,)), dma((g,)), dma((g,)),
        dma((n, 2)), dma((n, 2)), dma((n, 2)), dma((n, 2)), dma((n, 2)), dma((n, 2)),
        dma((n, 2)), dma((n, 2)), dma((n, 2)), dma((n, 2)), dma((n, 2)), dma((n, 2)),
        dma((2,)), dma((g,)), dma((2,)), dma((g,)), dma, dma,
    ]
    out = pl.pallas_call(
        kernel,
        out_shape=jax.ShapeDtypeStruct((2, HALF, D), F32),
        in_specs=[any_space, any_space, vmem, any_space],
        out_specs=vmem,
        scratch_shapes=scratch,
        compiler_params=pltpu.CompilerParams(collective_id=0, has_side_effects=True, vmem_limit_bytes=62 * 2**20),
        cost_estimate=pl.CostEstimate(flops=4 * 1024 * D * FF, bytes_accessed=4 * D * FF, transcendentals=1024 * QUARTER),
    )(tokens.reshape(2, HALF, D), w_in, b_in, w_out)
    return out.reshape(2 * HALF, D) + b_out.astype(F32)


def solution(mesh):
    return jax.shard_map(
        per_device,
        mesh=mesh,
        in_specs=(P("col", "row"), P("row", "col"), P("col"), P("col", "row"), P("row")),
        out_specs=P("col", "row"),
        check_vma=False,
    )
```

```python
import jax
import jax.numpy as jnp
from jax import lax
from jax.experimental import pallas as pl
from jax.experimental.pallas import tpu as pltpu
from jax.sharding import PartitionSpec as P

MESH = pl.DeviceIdType.MESH
F32, BF16 = jnp.float32, jnp.bfloat16
GROUPS, SLOTS = 8, 16
ROWS, SLOT, HALF = 128, 64, 32
D, FF = 1536, 3072
PAIR, QUARTER = 768, 384

HIDDEN_SCALE, OUT_SCALE = 2.0**20, 2.0**9

ORDER = (
    ("first", 0), ("sum_x1", 1), ("gather_y0", 5), ("second", 9), ("activate1", 3), ("sum_y1", 2), ("activate0", 2),
    ("gather_x1", 7), ("cross", 11), ("sum_y0", 1), ("sum_x0", 0), ("pass_on", -1), ("send_out", 9), ("gather_x0", 6),
    ("gather_y1", 5),
)
STEPS = 17


def code(v, scale):
    v = v * scale
    return ((v * v) * (v * jnp.abs(v))).astype(BF16)


def decode(coded, scale):
    y = coded.astype(F32)
    r = lax.rsqrt(jnp.maximum(jnp.abs(y), 1e-37))
    return y * (r * r) * (lax.rsqrt(r) * (1.0 / scale))


def kernel(tok_hbm, w1_hbm, bin_hbm, w2_hbm, bout_hbm, out_ref,
           w1, w2, bin_raw, bout_raw, bias_in, bias_out, tok, x1s, x1r, keep, ys, yr, x2s, x2r, hid, po, cr, osend, orecv, acc, y2s, y2r,
           w1_sem, w2_sem, bias_sem, own_sem, first_ss, tok_rs, relay_ss, fwd_ss, fwd_rs,
           x1_ss, x1_rs, y_ss, y_rs, x2_ss, x2_rs, gx_ss, gx_rs, gy_ss, gy_rs, gxx_ss, gxx_rs,
           c_ss, c_rs, o_ss, o_rs, y2_ss, y2_rs):
    row, col = lax.axis_index("row"), lax.axis_index("col")
    x, yh = row // 2, row % 2
    yl, z, core = col // 8, (col // 2) % 4, col % 2
    x_one = x + 1 - 2 * (x % 2)
    x_three = 3 - x
    one = (x_one * 2 + yh, col)
    three = (x_three * 2 + yh, col)
    across = (x * 2 + 1 - yh, col)
    sibling = (row, col + 1 - 2 * core)
    low = (row, (1 - yl) * 8 + z * 2 + core)

    def along_z(d):
        return (row, yl * 8 + ((z + d) % 4) * 2 + core)

    def cols(start, size):
        return pl.ds(pl.multiple_of(start, 128), size)

    def rows(start, size=HALF):
        return pl.ds(pl.multiple_of(start, HALF), size)

    mine = (((x + 1) // 2) % 2, x // 2)
    q = (x // 2, x % 2)
    pair_of = tuple(h * 2 * PAIR + mine[h] * PAIR for h in (0, 1))
    other_pair = tuple(h * 2 * PAIR + (1 - mine[h]) * PAIR for h in (0, 1))
    quarter_of = tuple(pair_of[h] + q[h] * QUARTER for h in (0, 1))
    kept = tuple(cols(q[h] * QUARTER, QUARTER) for h in (0, 1))
    gone = tuple(cols((1 - q[h]) * QUARTER, QUARTER) for h in (0, 1))
    dest1, dest2 = (one, three), (three, one)
    my_half, other_half = rows(yh * HALF), rows((1 - yh) * HALF)
    own_rows, other_rows = rows(core * HALF), rows((1 - core) * HALF)

    def remote(src, dst, ss, rs, dev):
        return pltpu.make_async_remote_copy(src_ref=src, dst_ref=dst, send_sem=ss, recv_sem=rs, device_id=dev, device_id_type=MESH)

    barrier = pltpu.get_barrier_semaphore()
    partners = [one, three, across, sibling, low] + [along_z(d) for d in (1, 2, 3)]
    for dev in partners:
        pl.semaphore_signal(barrier, inc=1, device_id=dev, device_id_type=MESH)

    w1_order = (other_pair[0], other_pair[1], pair_of[0], pair_of[1])

    def load_w1(i):
        c = cols(w1_order[i], PAIR)
        return pltpu.make_async_copy(w1_hbm.at[:, c], w1.at[:, c], w1_sem.at[i])

    own = pltpu.make_async_copy(tok_hbm, tok.at[0, :, own_rows], own_sem)
    own.start()
    for i in range(4):
        load_w1(i).start()
    load_bin = pltpu.make_async_copy(bin_hbm, bin_raw, bias_sem.at[0])
    load_bin.start()
    load_bout = pltpu.make_async_copy(bout_hbm, bout_raw, bias_sem.at[1])
    load_bout.start()
    load_w2 = pltpu.make_async_copy(w2_hbm, w2, w2_sem)

    pl.semaphore_wait(barrier, len(partners))

    near = {1: 1, 2: 6, 3: 7}

    def block(r):
        return tok.at[r, :, own_rows]

    def to_sibling(r):
        return remote(block(r), block(r), fwd_ss.at[r], fwd_rs.at[r], sibling)

    def from_sibling(r):
        return remote(tok.at[r, :, other_rows], tok.at[r, :, other_rows], fwd_ss.at[r], fwd_rs.at[r], sibling)

    own.wait()
    to_sibling(0).start()
    to_low = remote(block(0), block(2), first_ss.at[0], tok_rs.at[2], low)
    to_low.start()

    def to_z(d):
        return remote(block(0), block(near[d]), first_ss.at[d], tok_rs.at[near[d]], along_z(4 - d))

    to_z(1).start()

    def relay(d):
        return remote(block(2), block(2 + d), relay_ss.at[d - 1], tok_rs.at[2 + d], along_z(4 - d))

    def take(r):
        remote(block(r), block(r), fwd_ss.at[r], tok_rs.at[r], low).wait_recv()
        to_sibling(r).start()

    def pass_on(p):
        @pl.when(p == 1)
        def _():
            take(1)
            take(2)
            for d in (1, 3, 2):
                relay(d).start()
            for d in (3, 2):
                to_z(d).start()

        @pl.when((p > 1) & (p < GROUPS - 1))
        def _():
            take(p + 1)

    def x1_copy(k, h):
        return remote(x1s.at[k, h], x1r.at[k, h], x1_ss.at[k, h], x1_rs.at[k, h], dest1[h])

    def first(r):
        from_sibling(r).wait_recv()
        tokens = tok[r].reshape(ROWS, D)

        @pl.when(r == 1)
        def _():
            load_w2.start()
            load_bin.wait()
            load_bout.wait()
            bias_in[...] = bin_raw[...].astype(F32).reshape(1, FF)
            bias_out[...] = bout_raw[...].astype(F32).reshape(1, D)

        for i in range(4):
            h = i % 2

            @pl.when(r == 0)
            def _():
                load_w1(i).wait()

            part = jnp.dot(tokens, w1[:, cols(w1_order[i], PAIR)], preferred_element_type=F32)
            for u in (0, 1):
                if i < 2:
                    x1s[2 * r + u, h] = code(part[u * SLOT : (u + 1) * SLOT], HIDDEN_SCALE)
                    x1_copy(2 * r + u, h).start()
                else:
                    keep[2 * r + u, h] = part[u * SLOT : (u + 1) * SLOT]

    def y_copy(k, h):
        return remote(ys.at[k, h], yr.at[k, h], y_ss.at[k, h], y_rs.at[k, h], across)

    def sum_x(k):
        for h in (0, 1):
            x1_copy(k, h).wait_recv()
            ys[k, h] = code(keep[k, h, other_half] + decode(x1r[k, h, other_half], HIDDEN_SCALE), HIDDEN_SCALE)
            y_copy(k, h).start()
        for h in (0, 1):
            keep[k, h, my_half] += decode(x1r[k, h, my_half], HIDDEN_SCALE)

    def x2_copy(k, h):
        return remote(x2s.at[k, h], x2r.at[k, h], x2_ss.at[k, h], x2_rs.at[k, h], dest2[h])

    def sum_y(k):
        for h in (0, 1):
            y_copy(k, h).wait_recv()
            x2s[k, h] = code(keep[k, h, my_half, gone[h]] + decode(yr[k, h, :, gone[h]], HIDDEN_SCALE), HIDDEN_SCALE)
            x2_copy(k, h).start()
        for h in (0, 1):
            keep[k, h, my_half, kept[h]] += decode(yr[k, h, :, kept[h]], HIDDEN_SCALE)

    def hid_copy(k, which, start, size, ss, rs, dev):
        c = cols(start, size)
        return remote(hid.at[k, which, c], hid.at[k, which, c], ss, rs, dev)

    def gx_copy(k, h):
        return hid_copy(k, my_half, quarter_of[h], QUARTER, gx_ss.at[k, h], gx_rs.at[k, h], dest2[h])

    def gy_copy(k, h):
        return hid_copy(k, my_half, pair_of[h], PAIR, gy_ss.at[k, h], gy_rs.at[k, h], across)

    def gxx_copy(k, h):
        return hid_copy(k, pl.ds(0, SLOT), pair_of[h], PAIR, gxx_ss.at[k, h], gxx_rs.at[k, h], dest1[h])

    def activate(k):
        for h in (0, 1):
            x2_copy(k, h).wait_recv()
            c = cols(quarter_of[h], QUARTER)
            summed = keep[k, h, my_half, kept[h]] + decode(x2r[k, h], HIDDEN_SCALE)
            hid[k, my_half, c] = jax.nn.gelu(summed + bias_in[:, c], approximate=True).astype(BF16)
            gx_copy(k, h).start()

    def gather_y(k):
        for h in (0, 1):
            gx_copy(k, h).wait_recv()
            gy_copy(k, h).start()

    def gather_x(k):
        for h in (0, 1):
            gy_copy(k, h).wait_recv()
            gxx_copy(k, h).start()
        for h in (0, 1):
            x1_copy(k, h).wait_send()
            y_copy(k, h).wait_send()
            x2_copy(k, h).wait_send()

    def c_copy(m, i):
        r, c = (m + 1) % GROUPS, pl.ds(i * PAIR, PAIR)
        return remote(po.at[m % 2, :, other_rows, c], cr.at[r, :, :, c], c_ss.at[m % 2, i], c_rs.at[r, i], sibling)

    def second(m):
        r = (m + 1) % GROUPS

        @pl.when(m == 0)
        def _():
            load_w2.wait()

        @pl.when(m >= 2)
        def _():
            for i in (0, 1):
                c_copy(m - 2, i).wait_send()

        for u in (0, 1):
            for h in (0, 1):
                gxx_copy(2 * r + u, h).wait_recv()
        hidden = hid[pl.ds(2 * r, 2)].reshape(ROWS, FF)
        for i in (0, 1):
            c = pl.ds(i * PAIR, PAIR)
            po[m % 2, :, :, c] = jnp.dot(hidden, w2[:, c], preferred_element_type=F32).reshape(2, SLOT, PAIR)
            c_copy(m, i).start()
        for u in (0, 1):
            for h in (0, 1):
                gx_copy(2 * r + u, h).wait_send()
                gy_copy(2 * r + u, h).wait_send()

    def o_copy(m, i):
        r, c = (m + 1) % GROUPS, pl.ds(i * PAIR, PAIR)
        far = (r + 2) // 4 % 2
        return remote(osend.at[m % 2, :, :, c], orecv.at[r, :, :, c], o_ss.at[m % 2, i], o_rs.at[r, i], along_z((r + 2 * far) % 4))

    def send_out(m):
        r = (m + 1) % GROUPS
        for i in (0, 1):
            c = pl.ds(i * PAIR, PAIR)
            c_copy(m, i).wait_recv()

            @pl.when((m == 1) | (m == 7))
            def _():
                acc[m // 4, :, :, c] = po[m % 2, :, own_rows, c] + cr[r, :, :, c]

            @pl.when((m != 1) & (m != 7))
            def _():
                @pl.when(m == 2)
                def _():
                    o_copy(0, i).wait_send()

                @pl.when(m >= 4)
                def _():
                    o_copy(m - 2, i).wait_send()

                osend[m % 2, :, :, c] = code(po[m % 2, :, own_rows, c] + cr[r, :, :, c], OUT_SCALE)
                o_copy(m, i).start()

        to_sibling(r).wait_send()
        for u in (0, 1):
            for h in (0, 1):
                gxx_copy(2 * r + u, h).wait_send()

    y2_copy = remote(y2s, y2r, y2_ss, y2_rs, low)

    def cross(m):
        @pl.when(m == 4)
        def _():
            for r in (3, 4, 5):
                for i in (0, 1):
                    o_copy(r - 1, i).wait_recv()
            y2s[...] = code(acc[0] + sum(decode(orecv[r], OUT_SCALE) for r in (3, 4, 5)), OUT_SCALE)
            y2_copy.start()
            to_low.wait_send()
            for d in (1, 2, 3):
                to_z(d).wait_send()
                relay(d).wait_send()

    tasks = dict(first=first, pass_on=pass_on, sum_x=sum_x, sum_y=sum_y, activate=activate, gather_y=gather_y,
                 gather_x=gather_x, second=second, send_out=send_out, cross=cross)

    def step(s, _):
        for name, lag in ORDER:
            p = s - lag

            @pl.when((p >= 0) & (p < GROUPS))
            def _():
                if name[-1] in "01":
                    r = (p + 1) % GROUPS if name.startswith("gather") else p
                    tasks[name[:-1]](2 * r + int(name[-1]))
                else:
                    tasks[name](p)

        return 0

    lax.fori_loop(0, STEPS, step, 0)

    for r in (1, 6, 7):
        for i in (0, 1):
            o_copy(r - 1, i).wait_recv()
    y2_copy.wait_recv()
    far = sum(decode(orecv[r], OUT_SCALE) for r in (1, 6, 7))
    out_ref[...] = acc[1] + far + decode(y2r[...], OUT_SCALE) + bias_out[...]

    for i in (0, 1):
        for m in (GROUPS - 2, GROUPS - 1):
            c_copy(m, i).wait_send()
        for m in (5, 6):
            o_copy(m, i).wait_send()
    y2_copy.wait_send()


def per_device(tokens, w_in, b_in, w_out, b_out):
    any_space, vmem = pl.BlockSpec(memory_space=pl.ANY), pl.BlockSpec(memory_space=pltpu.VMEM)
    dma = pltpu.SemaphoreType.DMA
    g, n = GROUPS, SLOTS
    scratch = [
        pltpu.VMEM((D, FF), BF16), pltpu.VMEM((FF, D), BF16), pltpu.VMEM((FF,), BF16), pltpu.VMEM((D,), BF16), pltpu.VMEM((1, FF), F32), pltpu.VMEM((1, D), F32), pltpu.VMEM((g, 2, SLOT, D), BF16),
        pltpu.VMEM((n, 2, SLOT, PAIR), BF16), pltpu.VMEM((n, 2, SLOT, PAIR), BF16), pltpu.VMEM((n, 2, SLOT, PAIR), F32),
        pltpu.VMEM((n, 2, HALF, PAIR), BF16), pltpu.VMEM((n, 2, HALF, PAIR), BF16),
        pltpu.VMEM((n, 2, HALF, QUARTER), BF16), pltpu.VMEM((n, 2, HALF, QUARTER), BF16),
        pltpu.VMEM((n, SLOT, FF), BF16), pltpu.VMEM((2, 2, SLOT, D), F32), pltpu.VMEM((g, 2, HALF, D), F32),
        pltpu.VMEM((2, 2, HALF, D), BF16), pltpu.VMEM((g, 2, HALF, D), BF16), pltpu.VMEM((2, 2, HALF, D), F32),
        pltpu.VMEM((2, HALF, D), BF16), pltpu.VMEM((2, HALF, D), BF16),
        dma((4,)), dma, dma((2,)), dma, dma((4,)), dma((g,)), dma((3,)), dma((g,)), dma((g,)),
        dma((n, 2)), dma((n, 2)), dma((n, 2)), dma((n, 2)), dma((n, 2)), dma((n, 2)),
        dma((n, 2)), dma((n, 2)), dma((n, 2)), dma((n, 2)), dma((n, 2)), dma((n, 2)),
        dma((2, 2)), dma((g, 2)), dma((2, 2)), dma((g, 2)), dma, dma,
    ]
    out = pl.pallas_call(
        kernel,
        out_shape=pltpu.VMEM((2, HALF, D), F32),
        in_specs=[any_space] * 5,
        out_specs=vmem,
        scratch_shapes=scratch,
        compiler_params=pltpu.CompilerParams(collective_id=0, has_side_effects=True, vmem_limit_bytes=62 * 2**20),
        cost_estimate=pl.CostEstimate(flops=4 * 1024 * D * FF, bytes_accessed=4 * D * FF, transcendentals=1024 * QUARTER),
    )(tokens.reshape(2, HALF, D), w_in, b_in, w_out, b_out)
    return out.reshape(2 * HALF, D)


def solution(mesh):
    return jax.shard_map(
        per_device,
        mesh=mesh,
        in_specs=(P("col", "row"), P("row", "col"), P("col"), P("col", "row"), P("row")),
        out_specs=P("col", "row"),
        check_vma=False,
    )
```

```python
import jax
import jax.numpy as jnp
from jax import lax
from jax.experimental import pallas as pl
from jax.experimental.pallas import tpu as pltpu
from jax.sharding import PartitionSpec as P

MESH = pl.DeviceIdType.MESH
F32, BF16 = jnp.float32, jnp.bfloat16
GROUPS, SLOTS = 8, 16
ROWS, SLOT, HALF = 128, 64, 32
D, FF = 1536, 3072
PAIR, QUARTER = 768, 384

HIDDEN_SCALE, OUT_SCALE = 2.0**20, 2.0**9

ORDER = (
    ("send_out", 12), ("pass_on", 0), ("first", 0), ("second", 11), ("activate0", 4), ("sum_x0", 1), ("activate1", 4),
    ("gather_x0", 9), ("sum_y0", 2), ("sum_x1", 1), ("cross", 13), ("gather_x1", 8), ("gather_y0", 7), ("sum_y1", 2),
    ("gather_y1", 6),
)
STEPS = 20


def code(v, scale):
    v = v * scale
    return ((v * v) * (v * jnp.abs(v))).astype(BF16)


def decode(coded, scale):
    y = coded.astype(F32)
    r = lax.rsqrt(jnp.maximum(jnp.abs(y), 1e-37))
    return y * (r * r) * (lax.rsqrt(r) * (1.0 / scale))


def kernel(tok_hbm, w1_hbm, bin_hbm, w2_hbm, bout_hbm, out_ref,
           w1, w2, bin_raw, bout_raw, bias_in, bias_out, tok, x1s, x1r, keep, ys, yr, x2s, x2r, hid, po, cr, osend, orecv, acc, y2s, y2r,
           w1_sem, w2_sem, bias_sem, own_sem, first_ss, tok_rs, z_ss, fwd_ss, fwd_rs,
           x1_ss, x1_rs, y_ss, y_rs, x2_ss, x2_rs, gx_ss, gx_rs, gy_ss, gy_rs, gxx_ss, gxx_rs,
           c_ss, c_rs, o_ss, o_rs, y2_ss, y2_rs):
    row, col = lax.axis_index("row"), lax.axis_index("col")
    x, yh = row // 2, row % 2
    yl, z, core = col // 8, (col // 2) % 4, col % 2
    x_one = x + 1 - 2 * (x % 2)
    x_three = 3 - x
    one = (x_one * 2 + yh, col)
    three = (x_three * 2 + yh, col)
    across = (x * 2 + 1 - yh, col)
    sibling = (row, col + 1 - 2 * core)
    low = (row, (1 - yl) * 8 + z * 2 + core)

    def along_z(d):
        return (row, yl * 8 + ((z + d) % 4) * 2 + core)

    def cols(start, size):
        return pl.ds(pl.multiple_of(start, 128), size)

    def rows(start, size=HALF):
        return pl.ds(pl.multiple_of(start, HALF), size)

    mine = (((x + 1) // 2) % 2, x // 2)
    q = (x // 2, x % 2)
    pair_of = tuple(h * 2 * PAIR + mine[h] * PAIR for h in (0, 1))
    other_pair = tuple(h * 2 * PAIR + (1 - mine[h]) * PAIR for h in (0, 1))
    quarter_of = tuple(pair_of[h] + q[h] * QUARTER for h in (0, 1))
    kept = tuple(cols(q[h] * QUARTER, QUARTER) for h in (0, 1))
    gone = tuple(cols((1 - q[h]) * QUARTER, QUARTER) for h in (0, 1))
    dest1, dest2 = (one, three), (three, one)
    my_half, other_half = rows(yh * HALF), rows((1 - yh) * HALF)
    own_rows, other_rows = rows(core * HALF), rows((1 - core) * HALF)

    def remote(src, dst, ss, rs, dev):
        return pltpu.make_async_remote_copy(src_ref=src, dst_ref=dst, send_sem=ss, recv_sem=rs, device_id=dev, device_id_type=MESH)

    barrier = pltpu.get_barrier_semaphore()
    partners = [one, three, across, sibling, low] + [along_z(d) for d in (1, 2, 3)]
    for dev in partners:
        pl.semaphore_signal(barrier, inc=1, device_id=dev, device_id_type=MESH)

    w1_order = (other_pair[0], other_pair[1], pair_of[0], pair_of[1])

    def load_w1(i):
        c = cols(w1_order[i], PAIR)
        return pltpu.make_async_copy(w1_hbm.at[:, c], w1.at[:, c], w1_sem.at[i])

    own = pltpu.make_async_copy(tok_hbm, tok.at[0, :, own_rows], own_sem)
    own.start()
    for i in range(4):
        load_w1(i).start()
    load_bin = pltpu.make_async_copy(bin_hbm, bin_raw, bias_sem.at[0])
    load_bin.start()
    load_bout = pltpu.make_async_copy(bout_hbm, bout_raw, bias_sem.at[1])
    load_bout.start()
    load_w2 = pltpu.make_async_copy(w2_hbm, w2, w2_sem)

    pl.semaphore_wait(barrier, len(partners))

    def block(r):
        return tok.at[r, :, own_rows]

    def to_sibling(r):
        return remote(block(r), block(r), fwd_ss.at[r], fwd_rs.at[r], sibling)

    def from_sibling(r):
        return remote(tok.at[r, :, other_rows], tok.at[r, :, other_rows], fwd_ss.at[r], fwd_rs.at[r], sibling)

    own.wait()
    to_sibling(0).start()
    to_low = remote(block(0), block(2), first_ss, tok_rs.at[2], low)
    to_low.start()

    def along(side, d, u=None):
        src = 2 * side
        if d == 2:
            r = 6 - 2 * side
            return remote(block(src), block(r), z_ss.at[side, 4], tok_rs.at[r], along_z(2))
        r, i = ((1, 7), (3, 5))[side][u], d // 2
        return remote(tok.at[src, u, own_rows], tok.at[r, i, own_rows], z_ss.at[side, 2 * i + u], tok_rs.at[r], along_z(4 - d))

    along(0, 1, 0).start()
    along(0, 3, 0).start()

    def take(r):
        remote(block(r), block(r), fwd_ss.at[r], tok_rs.at[r], low).wait_recv()
        to_sibling(r).start()

    def pass_on(p):
        @pl.when(p == 1)
        def _():
            take(1)
            take(2)
            along(1, 1, 0).start()
            along(1, 3, 0).start()
            along(1, 2).start()

        @pl.when((p > 1) & (p < GROUPS - 1))
        def _():
            take(p + 1)

        @pl.when(p == 2)
        def _():
            along(1, 1, 1).start()
            along(1, 3, 1).start()
            along(0, 2).start()

        @pl.when(p == 3)
        def _():
            along(0, 1, 1).start()
            along(0, 3, 1).start()

    def x1_copy(k, h):
        return remote(x1s.at[k, h], x1r.at[k, h], x1_ss.at[k, h], x1_rs.at[k, h], dest1[h])

    def first(r):
        from_sibling(r).wait_recv()
        tokens = tok[r].reshape(ROWS, D)

        @pl.when(r == 1)
        def _():
            load_w2.start()
            load_bin.wait()
            load_bout.wait()
            bias_in[...] = bin_raw[...].astype(F32).reshape(1, FF)
            bias_out[...] = bout_raw[...].astype(F32).reshape(1, D)

        for i in range(4):
            h = i % 2

            @pl.when(r == 0)
            def _():
                load_w1(i).wait()

            part = jnp.dot(tokens, w1[:, cols(w1_order[i], PAIR)], preferred_element_type=F32)
            for u in (0, 1):
                if i < 2:
                    x1s[2 * r + u, h] = code(part[u * SLOT : (u + 1) * SLOT], HIDDEN_SCALE)
                    x1_copy(2 * r + u, h).start()
                else:
                    keep[2 * r + u, h] = part[u * SLOT : (u + 1) * SLOT]

    def y_copy(k, h):
        return remote(ys.at[k, h], yr.at[k, h], y_ss.at[k, h], y_rs.at[k, h], across)

    def sum_x(k):
        for h in (0, 1):
            x1_copy(k, h).wait_recv()
            ys[k, h] = code(keep[k, h, other_half] + decode(x1r[k, h, other_half], HIDDEN_SCALE), HIDDEN_SCALE)
            y_copy(k, h).start()
        for h in (0, 1):
            keep[k, h, my_half] += decode(x1r[k, h, my_half], HIDDEN_SCALE)

    def x2_copy(k, h):
        return remote(x2s.at[k, h], x2r.at[k, h], x2_ss.at[k, h], x2_rs.at[k, h], dest2[h])

    def sum_y(k):
        for h in (0, 1):
            y_copy(k, h).wait_recv()
            x2s[k, h] = code(keep[k, h, my_half, gone[h]] + decode(yr[k, h, :, gone[h]], HIDDEN_SCALE), HIDDEN_SCALE)
            x2_copy(k, h).start()
        for h in (0, 1):
            keep[k, h, my_half, kept[h]] += decode(yr[k, h, :, kept[h]], HIDDEN_SCALE)

    def hid_copy(k, which, start, size, ss, rs, dev):
        c = cols(start, size)
        return remote(hid.at[k, which, c], hid.at[k, which, c], ss, rs, dev)

    def gx_copy(k, h):
        return hid_copy(k, my_half, quarter_of[h], QUARTER, gx_ss.at[k, h], gx_rs.at[k, h], dest2[h])

    def gy_copy(k, h):
        return hid_copy(k, my_half, pair_of[h], PAIR, gy_ss.at[k, h], gy_rs.at[k, h], across)

    def gxx_copy(k, h):
        return hid_copy(k, pl.ds(0, SLOT), pair_of[h], PAIR, gxx_ss.at[k, h], gxx_rs.at[k, h], dest1[h])

    def activate(k):
        for h in (0, 1):
            x2_copy(k, h).wait_recv()
            c = cols(quarter_of[h], QUARTER)
            summed = keep[k, h, my_half, kept[h]] + decode(x2r[k, h], HIDDEN_SCALE)
            hid[k, my_half, c] = jax.nn.gelu(summed + bias_in[:, c], approximate=True).astype(BF16)
            gx_copy(k, h).start()

    def gather_y(k):
        for h in (0, 1):
            gx_copy(k, h).wait_recv()
            gy_copy(k, h).start()

    def gather_x(k):
        for h in (0, 1):
            gy_copy(k, h).wait_recv()
            gxx_copy(k, h).start()
        for h in (0, 1):
            x1_copy(k, h).wait_send()
            y_copy(k, h).wait_send()
            x2_copy(k, h).wait_send()

    def c_copy(m, i):
        r, c = (m + 1) % GROUPS, pl.ds(i * PAIR, PAIR)
        return remote(po.at[m % 2, :, other_rows, c], cr.at[r, :, :, c], c_ss.at[m % 2, i], c_rs.at[r, i], sibling)

    def second(m):
        r = (m + 1) % GROUPS

        @pl.when(m == 0)
        def _():
            load_w2.wait()

        @pl.when(m >= 2)
        def _():
            for i in (0, 1):
                c_copy(m - 2, i).wait_send()

        for u in (0, 1):
            for h in (0, 1):
                gxx_copy(2 * r + u, h).wait_recv()
        hidden = hid[pl.ds(2 * r, 2)].reshape(ROWS, FF)
        for i in (0, 1):
            c = pl.ds(i * PAIR, PAIR)
            po[m % 2, :, :, c] = jnp.dot(hidden, w2[:, c], preferred_element_type=F32).reshape(2, SLOT, PAIR)
            c_copy(m, i).start()
        for u in (0, 1):
            for h in (0, 1):
                gx_copy(2 * r + u, h).wait_send()
                gy_copy(2 * r + u, h).wait_send()

    def o_copy(m, u):
        r = (m + 1) % GROUPS
        d = 2 + r % 2 * (2 * u - 1)
        return remote(osend.at[m % 2, u], orecv.at[r, u], o_ss.at[m % 2, u], o_rs.at[r, u], along_z(d))

    def send_out(m):
        r = (m + 1) % GROUPS
        for i in (0, 1):
            c_copy(m, i).wait_recv()

        @pl.when((m == 1) | (m == 7))
        def _():
            acc[m // 4] = po[m % 2, :, own_rows] + cr[r]

        @pl.when((m != 1) & (m != 7))
        def _():
            for u in (0, 1):
                @pl.when(m == 2)
                def _():
                    o_copy(0, u).wait_send()

                @pl.when(m >= 4)
                def _():
                    o_copy(m - 2, u).wait_send()

                osend[m % 2, u] = code(po[m % 2, u, own_rows] + cr[r, u], OUT_SCALE)
                o_copy(m, u).start()

        to_sibling(r).wait_send()
        for u in (0, 1):
            for h in (0, 1):
                gxx_copy(2 * r + u, h).wait_send()

    def y2_copy(u):
        return remote(y2s.at[u], y2r.at[u], y2_ss.at[u], y2_rs.at[u], low)

    def others(u, a, b, c):
        r = c if u else a
        for i in (0, 1):
            o_copy(r - 1, i).wait_recv()
        o_copy(b - 1, u).wait_recv()
        return decode(orecv[r, 0], OUT_SCALE) + decode(orecv[r, 1], OUT_SCALE) + decode(orecv[b, u], OUT_SCALE)

    def cross(m):
        for u in (0, 1):
            @pl.when(m == 3 + u)
            def _():
                y2s[u] = code(acc[0, u] + others(u, 3, 4, 5), OUT_SCALE)
                y2_copy(u).start()

        @pl.when(m == 4)
        def _():
            to_low.wait_send()
            for side in (0, 1):
                for d in (1, 3):
                    for u in (0, 1):
                        along(side, d, u).wait_send()
                along(side, 2).wait_send()

    tasks = dict(first=first, pass_on=pass_on, sum_x=sum_x, sum_y=sum_y, activate=activate, gather_y=gather_y,
                 gather_x=gather_x, second=second, send_out=send_out, cross=cross)

    def step(s, _):
        for name, lag in ORDER:
            p = s - lag

            @pl.when((p >= 0) & (p < GROUPS))
            def _():
                if name[-1] in "01":
                    r = (p + 1) % GROUPS if name.startswith("gather") else p
                    tasks[name[:-1]](2 * r + int(name[-1]))
                else:
                    tasks[name](p)

        return 0

    lax.fori_loop(0, STEPS, step, 0)

    for u in (0, 1):
        y2_copy(u).wait_recv()
        rest = acc[1, u] + decode(y2r[u], OUT_SCALE) + bias_out[...]
        out_ref[u] = rest + others(u, 1, 6, 7)

    for i in (0, 1):
        for m in (GROUPS - 2, GROUPS - 1):
            c_copy(m, i).wait_send()
        for m in (5, 6):
            o_copy(m, i).wait_send()
    for u in (0, 1):
        y2_copy(u).wait_send()


def per_device(tokens, w_in, b_in, w_out, b_out):
    any_space, vmem = pl.BlockSpec(memory_space=pl.ANY), pl.BlockSpec(memory_space=pltpu.VMEM)
    dma = pltpu.SemaphoreType.DMA
    g, n = GROUPS, SLOTS
    scratch = [
        pltpu.VMEM((D, FF), BF16), pltpu.VMEM((FF, D), BF16), pltpu.VMEM((FF,), BF16), pltpu.VMEM((D,), BF16), pltpu.VMEM((1, FF), F32), pltpu.VMEM((1, D), F32), pltpu.VMEM((g, 2, SLOT, D), BF16),
        pltpu.VMEM((n, 2, SLOT, PAIR), BF16), pltpu.VMEM((n, 2, SLOT, PAIR), BF16), pltpu.VMEM((n, 2, SLOT, PAIR), F32),
        pltpu.VMEM((n, 2, HALF, PAIR), BF16), pltpu.VMEM((n, 2, HALF, PAIR), BF16),
        pltpu.VMEM((n, 2, HALF, QUARTER), BF16), pltpu.VMEM((n, 2, HALF, QUARTER), BF16),
        pltpu.VMEM((n, SLOT, FF), BF16), pltpu.VMEM((2, 2, SLOT, D), F32), pltpu.VMEM((g, 2, HALF, D), F32),
        pltpu.VMEM((2, 2, HALF, D), BF16), pltpu.VMEM((g, 2, HALF, D), BF16), pltpu.VMEM((2, 2, HALF, D), F32),
        pltpu.VMEM((2, HALF, D), BF16), pltpu.VMEM((2, HALF, D), BF16),
        dma((4,)), dma, dma((2,)), dma, dma, dma((g,)), dma((2, 5)), dma((g,)), dma((g,)),
        dma((n, 2)), dma((n, 2)), dma((n, 2)), dma((n, 2)), dma((n, 2)), dma((n, 2)),
        dma((n, 2)), dma((n, 2)), dma((n, 2)), dma((n, 2)), dma((n, 2)), dma((n, 2)),
        dma((2, 2)), dma((g, 2)), dma((2, 2)), dma((g, 2)), dma((2,)), dma((2,)),
    ]
    out = pl.pallas_call(
        kernel,
        out_shape=pltpu.VMEM((2, HALF, D), F32),
        in_specs=[any_space] * 5,
        out_specs=vmem,
        scratch_shapes=scratch,
        compiler_params=pltpu.CompilerParams(collective_id=0, has_side_effects=True, vmem_limit_bytes=62 * 2**20),
        cost_estimate=pl.CostEstimate(flops=4 * 1024 * D * FF, bytes_accessed=4 * D * FF, transcendentals=1024 * QUARTER),
    )(tokens.reshape(2, HALF, D), w_in, b_in, w_out, b_out)
    return out.reshape(2 * HALF, D)


def solution(mesh):
    return jax.shard_map(
        per_device,
        mesh=mesh,
        in_specs=(P("col", "row"), P("row", "col"), P("col"), P("col", "row"), P("row")),
        out_specs=P("col", "row"),
        check_vma=False,
    )
```

```python
import jax
import jax.numpy as jnp
from jax import lax
from jax.experimental import pallas as pl
from jax.experimental.pallas import tpu as pltpu
from jax.sharding import PartitionSpec as P

MESH = pl.DeviceIdType.MESH
F32, BF16 = jnp.float32, jnp.bfloat16
GROUPS, SLOTS = 8, 16
ROWS, SLOT, HALF = 128, 64, 32
D, FF = 1536, 3072
PAIR, QUARTER = 768, 384

HIDDEN_SCALE, OUT_SCALE = 2.0**20, 2.0**9

ORDER = (
    ("gather_y0", 6), ("first", 0), ("gather_x1", 8), ("sum_x0", 1), ("sum_y0", 2), ("cross", 12), ("sum_x1", 1),
    ("send_out", 10), ("pass_on", -1), ("activate0", 3), ("gather_y1", 6), ("gather_x0", 7), ("second", 9),
    ("sum_y1", 2), ("activate1", 3),
)
STEPS = 18


def code(v, scale):
    v = v * scale
    return ((v * v) * (v * jnp.abs(v))).astype(BF16)


def decode(coded, scale):
    y = coded.astype(F32)
    r = lax.rsqrt(jnp.maximum(jnp.abs(y), 1e-37))
    return y * (r * r) * (lax.rsqrt(r) * (1.0 / scale))


def kernel(tok_hbm, w1_hbm, bin_hbm, w2_hbm, bout_hbm, out_ref,
           w1, w2, bin_raw, bout_raw, bias_in, bias_out, tok, x1s, x1r, keep, ys, yr, x2s, x2r, hid, po, cr, osend, orecv, acc, y2s, y2r,
           w1_sem, w2_sem, bias_sem, own_sem, low_ss, low_rs, tok_rs, z_ss, fwd_ss, fwd_rs,
           x1_ss, x1_rs, y_ss, y_rs, x2_ss, x2_rs, gx_ss, gx_rs, gy_ss, gy_rs, gxx_ss, gxx_rs,
           c_ss, c_rs, o_ss, o_rs, y2_ss, y2_rs):
    row, col = lax.axis_index("row"), lax.axis_index("col")
    x, yh = row // 2, row % 2
    yl, z, core = col // 8, (col // 2) % 4, col % 2
    x_one = x + 1 - 2 * (x % 2)
    x_three = 3 - x
    one = (x_one * 2 + yh, col)
    three = (x_three * 2 + yh, col)
    across = (x * 2 + 1 - yh, col)
    sibling = (row, col + 1 - 2 * core)
    low = (row, (1 - yl) * 8 + z * 2 + core)

    def along_z(d):
        return (row, yl * 8 + ((z + d) % 4) * 2 + core)

    def cols(start, size):
        return pl.ds(pl.multiple_of(start, 128), size)

    def rows(start, size=HALF):
        return pl.ds(pl.multiple_of(start, HALF), size)

    mine = (((x + 1) // 2) % 2, x // 2)
    q = (x // 2, x % 2)
    pair_of = tuple(h * 2 * PAIR + mine[h] * PAIR for h in (0, 1))
    other_pair = tuple(h * 2 * PAIR + (1 - mine[h]) * PAIR for h in (0, 1))
    quarter_of = tuple(pair_of[h] + q[h] * QUARTER for h in (0, 1))
    kept = tuple(cols(q[h] * QUARTER, QUARTER) for h in (0, 1))
    gone = tuple(cols((1 - q[h]) * QUARTER, QUARTER) for h in (0, 1))
    dest1, dest2 = (one, three), (three, one)
    my_half, other_half = rows(yh * HALF), rows((1 - yh) * HALF)
    own_rows, other_rows = rows(core * HALF), rows((1 - core) * HALF)

    def remote(src, dst, ss, rs, dev):
        return pltpu.make_async_remote_copy(src_ref=src, dst_ref=dst, send_sem=ss, recv_sem=rs, device_id=dev, device_id_type=MESH)

    barrier = pltpu.get_barrier_semaphore()
    partners = [one, three, across, sibling, low] + [along_z(d) for d in (1, 2, 3)]
    for dev in partners:
        pl.semaphore_signal(barrier, inc=1, device_id=dev, device_id_type=MESH)

    w1_order = (other_pair[0], other_pair[1], pair_of[0], pair_of[1])

    def load_w1(i):
        c = cols(w1_order[i], PAIR)
        return pltpu.make_async_copy(w1_hbm.at[:, c], w1.at[:, c], w1_sem.at[i])

    own = pltpu.make_async_copy(tok_hbm, tok.at[0, :, own_rows], own_sem)
    own.start()
    for i in range(4):
        load_w1(i).start()
    load_bin = pltpu.make_async_copy(bin_hbm, bin_raw, bias_sem.at[0])
    load_bin.start()
    load_bout = pltpu.make_async_copy(bout_hbm, bout_raw, bias_sem.at[1])
    load_bout.start()
    load_w2 = pltpu.make_async_copy(w2_hbm, w2, w2_sem)

    pl.semaphore_wait(barrier, len(partners))

    def block(r):
        return tok.at[r, :, own_rows]

    def to_sibling(r):
        return remote(block(r), block(r), fwd_ss.at[r], fwd_rs.at[r], sibling)

    def from_sibling(r):
        return remote(tok.at[r, :, other_rows], tok.at[r, :, other_rows], fwd_ss.at[r], fwd_rs.at[r], sibling)

    own.wait()
    to_sibling(0).start()

    def to_low(u):
        return remote(tok.at[0, u, own_rows], tok.at[2, u, own_rows], low_ss.at[u], low_rs.at[u], low)

    for u in (0, 1):
        to_low(u).start()

    def along(side, d, u=None):
        src = 2 * side
        if d == 2:
            r = 6 - 2 * side
            return remote(block(src), block(r), z_ss.at[side, 4], tok_rs.at[r], along_z(2))
        r, i = ((1, 7), (3, 5))[side][u], d // 2
        return remote(tok.at[src, u, own_rows], tok.at[r, i, own_rows], z_ss.at[side, 2 * i + u], tok_rs.at[r], along_z(4 - d))

    along(0, 1, 0).start()
    along(0, 3, 0).start()

    def take(r):
        remote(block(r), block(r), fwd_ss.at[r], tok_rs.at[r], low).wait_recv()
        to_sibling(r).start()

    def pass_on(p):
        @pl.when(p == 1)
        def _():
            take(1)
            to_low(0).wait_recv()
            along(1, 1, 0).start()
            along(1, 3, 0).start()

        @pl.when((p > 1) & (p < GROUPS - 1))
        def _():
            take(p + 1)

        @pl.when(p == 2)
        def _():
            along(1, 1, 1).start()
            along(1, 3, 1).start()
            along(0, 2).start()

        @pl.when(p == 3)
        def _():
            along(0, 1, 1).start()
            along(0, 3, 1).start()

    def x1_copy(k, h):
        return remote(x1s.at[k, h], x1r.at[k, h], x1_ss.at[k, h], x1_rs.at[k, h], dest1[h])

    def first(r):
        from_sibling(r).wait_recv()
        tokens = tok[r].reshape(ROWS, D)

        @pl.when(r == 1)
        def _():
            load_w2.start()
            load_bin.wait()
            load_bout.wait()
            bias_in[...] = bin_raw[...].astype(F32).reshape(1, FF)
            bias_out[...] = bout_raw[...].astype(F32).reshape(1, D)

        for i in range(4):
            h = i % 2

            @pl.when(r == 0)
            def _():
                load_w1(i).wait()

            part = jnp.dot(tokens, w1[:, cols(w1_order[i], PAIR)], preferred_element_type=F32)
            for u in (0, 1):
                if i < 2:
                    x1s[2 * r + u, h] = code(part[u * SLOT : (u + 1) * SLOT], HIDDEN_SCALE)
                    x1_copy(2 * r + u, h).start()
                else:
                    keep[2 * r + u, h] = part[u * SLOT : (u + 1) * SLOT]

        @pl.when(r == 1)
        def _():
            to_low(1).wait_recv()
            to_sibling(2).start()
            along(1, 2).start()

    def y_copy(k, h):
        return remote(ys.at[k, h], yr.at[k, h], y_ss.at[k, h], y_rs.at[k, h], across)

    def sum_x(k):
        for h in (0, 1):
            x1_copy(k, h).wait_recv()
            ys[k, h] = code(keep[k, h, other_half] + decode(x1r[k, h, other_half], HIDDEN_SCALE), HIDDEN_SCALE)
            y_copy(k, h).start()
        for h in (0, 1):
            keep[k, h, my_half] += decode(x1r[k, h, my_half], HIDDEN_SCALE)

    def x2_copy(k, h):
        return remote(x2s.at[k, h], x2r.at[k, h], x2_ss.at[k, h], x2_rs.at[k, h], dest2[h])

    def sum_y(k):
        for h in (0, 1):
            y_copy(k, h).wait_recv()
            x2s[k, h] = code(keep[k, h, my_half, gone[h]] + decode(yr[k, h, :, gone[h]], HIDDEN_SCALE), HIDDEN_SCALE)
            x2_copy(k, h).start()
        for h in (0, 1):
            keep[k, h, my_half, kept[h]] += decode(yr[k, h, :, kept[h]], HIDDEN_SCALE)

    def hid_copy(k, which, start, size, ss, rs, dev):
        c = cols(start, size)
        return remote(hid.at[k, which, c], hid.at[k, which, c], ss, rs, dev)

    def gx_copy(k, h):
        return hid_copy(k, my_half, quarter_of[h], QUARTER, gx_ss.at[k, h], gx_rs.at[k, h], dest2[h])

    def gy_copy(k, h):
        return hid_copy(k, my_half, pair_of[h], PAIR, gy_ss.at[k, h], gy_rs.at[k, h], across)

    def gxx_copy(k, h):
        return hid_copy(k, pl.ds(0, SLOT), pair_of[h], PAIR, gxx_ss.at[k, h], gxx_rs.at[k, h], dest1[h])

    def activate(k):
        for h in (0, 1):
            x2_copy(k, h).wait_recv()
            c = cols(quarter_of[h], QUARTER)
            summed = keep[k, h, my_half, kept[h]] + decode(x2r[k, h], HIDDEN_SCALE)
            hid[k, my_half, c] = jax.nn.gelu(summed + bias_in[:, c], approximate=True).astype(BF16)
            gx_copy(k, h).start()

    def gather_y(k):
        for h in (0, 1):
            gx_copy(k, h).wait_recv()
            gy_copy(k, h).start()

    def gather_x(k):
        for h in (0, 1):
            gy_copy(k, h).wait_recv()
            gxx_copy(k, h).start()
        for h in (0, 1):
            x1_copy(k, h).wait_send()
            y_copy(k, h).wait_send()
            x2_copy(k, h).wait_send()

    def c_copy(m, i):
        r, c = (m + 1) % GROUPS, pl.ds(i * PAIR, PAIR)
        return remote(po.at[m % 2, :, other_rows, c], cr.at[r, :, :, c], c_ss.at[m % 2, i], c_rs.at[r, i], sibling)

    def second(m):
        r = (m + 1) % GROUPS

        @pl.when(m == 0)
        def _():
            load_w2.wait()

        @pl.when(m >= 2)
        def _():
            for i in (0, 1):
                c_copy(m - 2, i).wait_send()

        for u in (0, 1):
            for h in (0, 1):
                gxx_copy(2 * r + u, h).wait_recv()
        hidden = hid[pl.ds(2 * r, 2)].reshape(ROWS, FF)
        for i in (0, 1):
            c = pl.ds(i * PAIR, PAIR)
            po[m % 2, :, :, c] = jnp.dot(hidden, w2[:, c], preferred_element_type=F32).reshape(2, SLOT, PAIR)
            c_copy(m, i).start()
        for u in (0, 1):
            for h in (0, 1):
                gx_copy(2 * r + u, h).wait_send()
                gy_copy(2 * r + u, h).wait_send()

    def o_copy(m, u):
        r = (m + 1) % GROUPS
        d = 2 + r % 2 * (2 * u - 1)
        return remote(osend.at[m % 2, u], orecv.at[r, u], o_ss.at[m % 2, u], o_rs.at[r, u], along_z(d))

    def send_out(m):
        r = (m + 1) % GROUPS
        for i in (0, 1):
            c_copy(m, i).wait_recv()

        @pl.when((m == 1) | (m == 7))
        def _():
            acc[m // 4] = po[m % 2, :, own_rows] + cr[r]

        @pl.when((m != 1) & (m != 7))
        def _():
            for u in (0, 1):
                @pl.when(m == 2)
                def _():
                    o_copy(0, u).wait_send()

                @pl.when(m >= 4)
                def _():
                    o_copy(m - 2, u).wait_send()

                osend[m % 2, u] = code(po[m % 2, u, own_rows] + cr[r, u], OUT_SCALE)
                o_copy(m, u).start()

        to_sibling(r).wait_send()
        for u in (0, 1):
            for h in (0, 1):
                gxx_copy(2 * r + u, h).wait_send()

    def y2_copy(u):
        return remote(y2s.at[u], y2r.at[u], y2_ss.at[u], y2_rs.at[u], low)

    def others(u, a, b, c):
        r = c if u else a
        for i in (0, 1):
            o_copy(r - 1, i).wait_recv()
        o_copy(b - 1, u).wait_recv()
        return decode(orecv[r, 0], OUT_SCALE) + decode(orecv[r, 1], OUT_SCALE) + decode(orecv[b, u], OUT_SCALE)

    def cross(m):
        for u in (0, 1):
            @pl.when(m == 3 + u)
            def _():
                y2s[u] = code(acc[0, u] + others(u, 3, 4, 5), OUT_SCALE)
                y2_copy(u).start()

        @pl.when(m == 4)
        def _():
            for u in (0, 1):
                to_low(u).wait_send()
            for side in (0, 1):
                for d in (1, 3):
                    for u in (0, 1):
                        along(side, d, u).wait_send()
                along(side, 2).wait_send()

    tasks = dict(first=first, pass_on=pass_on, sum_x=sum_x, sum_y=sum_y, activate=activate, gather_y=gather_y,
                 gather_x=gather_x, second=second, send_out=send_out, cross=cross)

    def step(s, _):
        for name, lag in ORDER:
            p = s - lag

            @pl.when((p >= 0) & (p < GROUPS))
            def _():
                if name[-1] in "01":
                    r = (p + 1) % GROUPS if name.startswith("gather") else p
                    tasks[name[:-1]](2 * r + int(name[-1]))
                else:
                    tasks[name](p)

        return 0

    lax.fori_loop(0, STEPS, step, 0)

    for u in (0, 1):
        y2_copy(u).wait_recv()
        rest = acc[1, u] + decode(y2r[u], OUT_SCALE) + bias_out[...]
        out_ref[u] = rest + others(u, 1, 6, 7)

    for i in (0, 1):
        for m in (GROUPS - 2, GROUPS - 1):
            c_copy(m, i).wait_send()
        for m in (5, 6):
            o_copy(m, i).wait_send()
    for u in (0, 1):
        y2_copy(u).wait_send()


def per_device(tokens, w_in, b_in, w_out, b_out):
    any_space, vmem = pl.BlockSpec(memory_space=pl.ANY), pl.BlockSpec(memory_space=pltpu.VMEM)
    dma = pltpu.SemaphoreType.DMA
    g, n = GROUPS, SLOTS
    scratch = [
        pltpu.VMEM((D, FF), BF16), pltpu.VMEM((FF, D), BF16), pltpu.VMEM((FF,), BF16), pltpu.VMEM((D,), BF16), pltpu.VMEM((1, FF), F32), pltpu.VMEM((1, D), F32), pltpu.VMEM((g, 2, SLOT, D), BF16),
        pltpu.VMEM((n, 2, SLOT, PAIR), BF16), pltpu.VMEM((n, 2, SLOT, PAIR), BF16), pltpu.VMEM((n, 2, SLOT, PAIR), F32),
        pltpu.VMEM((n, 2, HALF, PAIR), BF16), pltpu.VMEM((n, 2, HALF, PAIR), BF16),
        pltpu.VMEM((n, 2, HALF, QUARTER), BF16), pltpu.VMEM((n, 2, HALF, QUARTER), BF16),
        pltpu.VMEM((n, SLOT, FF), BF16), pltpu.VMEM((2, 2, SLOT, D), F32), pltpu.VMEM((g, 2, HALF, D), F32),
        pltpu.VMEM((2, 2, HALF, D), BF16), pltpu.VMEM((g, 2, HALF, D), BF16), pltpu.VMEM((2, 2, HALF, D), F32),
        pltpu.VMEM((2, HALF, D), BF16), pltpu.VMEM((2, HALF, D), BF16),
        dma((4,)), dma, dma((2,)), dma, dma((2,)), dma((2,)), dma((g,)), dma((2, 5)), dma((g,)), dma((g,)),
        dma((n, 2)), dma((n, 2)), dma((n, 2)), dma((n, 2)), dma((n, 2)), dma((n, 2)),
        dma((n, 2)), dma((n, 2)), dma((n, 2)), dma((n, 2)), dma((n, 2)), dma((n, 2)),
        dma((2, 2)), dma((g, 2)), dma((2, 2)), dma((g, 2)), dma((2,)), dma((2,)),
    ]
    out = pl.pallas_call(
        kernel,
        out_shape=pltpu.VMEM((2, HALF, D), F32),
        in_specs=[any_space] * 5,
        out_specs=vmem,
        scratch_shapes=scratch,
        compiler_params=pltpu.CompilerParams(collective_id=0, has_side_effects=True, vmem_limit_bytes=62 * 2**20),
        cost_estimate=pl.CostEstimate(flops=4 * 1024 * D * FF, bytes_accessed=4 * D * FF, transcendentals=1024 * QUARTER),
    )(tokens.reshape(2, HALF, D), w_in, b_in, w_out, b_out)
    return out.reshape(2 * HALF, D)


def solution(mesh):
    return jax.shard_map(
        per_device,
        mesh=mesh,
        in_specs=(P("col", "row"), P("row", "col"), P("col"), P("col", "row"), P("row")),
        out_specs=P("col", "row"),
        check_vma=False,
    )
```

```python
import jax
import jax.numpy as jnp
from jax import lax
from jax.experimental import pallas as pl
from jax.experimental.pallas import tpu as pltpu
from jax.sharding import PartitionSpec as P

MESH = pl.DeviceIdType.MESH
F32, BF16 = jnp.float32, jnp.bfloat16
GROUPS, SLOTS = 8, 16
ROWS, SLOT, HALF = 128, 64, 32
D, FF = 1536, 3072
PAIR, QUARTER = 768, 384

HIDDEN_SCALE, OUT_SCALE = 2.0**20, 2.0**9

ORDER = (
    ("gather_y0", 6), ("first", 0), ("gather_x0", 8), ("sum_x0", 1), ("second", 10), ("sum_y1", 3), ("activate1", 4),
    ("gather_x1", 8), ("cross", 12), ("sum_x1", 1), ("sum_y0", 2), ("send_out", 10), ("pass_on", -1),
    ("activate0", 3), ("gather_y1", 6),
)
STEPS = 18


def code(v, scale):
    v = v * scale
    return ((v * v) * (v * jnp.abs(v))).astype(BF16)


def decode(coded, scale):
    y = coded.astype(F32)
    r = lax.rsqrt(jnp.maximum(jnp.abs(y), 1e-37))
    return y * (r * r) * (lax.rsqrt(r) * (1.0 / scale))


def kernel(tok_hbm, w1_hbm, bin_hbm, w2_hbm, bout_hbm, out_ref,
           w1, w2, bin_raw, bout_raw, bias_in, bias_out, tok, x1s, x1r, keep, ys, yr, x2s, x2r, hid, po, cr, osend, orecv, acc, y2s, y2r,
           w1_sem, w2_sem, bias_sem, own_sem, low_ss, low_rs, tok_rs, z_ss, fwd_ss, fwd_rs,
           x1_ss, x1_rs, y_ss, y_rs, x2_ss, x2_rs, gx_ss, gx_rs, gy_ss, gy_rs, gxx_ss, gxx_rs,
           c_ss, c_rs, o_ss, o_rs, y2_ss, y2_rs):
    row, col = lax.axis_index("row"), lax.axis_index("col")
    x, yh = row // 2, row % 2
    yl, z, core = col // 8, (col // 2) % 4, col % 2
    x_one = x + 1 - 2 * (x % 2)
    x_three = 3 - x
    one = (x_one * 2 + yh, col)
    three = (x_three * 2 + yh, col)
    across = (x * 2 + 1 - yh, col)
    sibling = (row, col + 1 - 2 * core)
    low = (row, (1 - yl) * 8 + z * 2 + core)

    def along_z(d):
        return (row, yl * 8 + ((z + d) % 4) * 2 + core)

    def cols(start, size):
        return pl.ds(pl.multiple_of(start, 128), size)

    def rows(start, size=HALF):
        return pl.ds(pl.multiple_of(start, HALF), size)

    mine = (((x + 1) // 2) % 2, x // 2)
    q = (x // 2, x % 2)
    pair_of = tuple(h * 2 * PAIR + mine[h] * PAIR for h in (0, 1))
    other_pair = tuple(h * 2 * PAIR + (1 - mine[h]) * PAIR for h in (0, 1))
    quarter_of = tuple(pair_of[h] + q[h] * QUARTER for h in (0, 1))
    kept = tuple(cols(q[h] * QUARTER, QUARTER) for h in (0, 1))
    gone = tuple(cols((1 - q[h]) * QUARTER, QUARTER) for h in (0, 1))
    dest1, dest2 = (one, three), (three, one)
    my_half, other_half = rows(yh * HALF), rows((1 - yh) * HALF)
    own_rows, other_rows = rows(core * HALF), rows((1 - core) * HALF)

    def remote(src, dst, ss, rs, dev):
        return pltpu.make_async_remote_copy(src_ref=src, dst_ref=dst, send_sem=ss, recv_sem=rs, device_id=dev, device_id_type=MESH)

    barrier = pltpu.get_barrier_semaphore()
    partners = [one, three, across, sibling, low] + [along_z(d) for d in (1, 2, 3)]
    for dev in partners:
        pl.semaphore_signal(barrier, inc=1, device_id=dev, device_id_type=MESH)

    w1_order = (other_pair[0], other_pair[1], pair_of[0], pair_of[1])

    def load_w1(i):
        c = cols(w1_order[i], PAIR)
        return pltpu.make_async_copy(w1_hbm.at[:, c], w1.at[:, c], w1_sem.at[i])

    own = pltpu.make_async_copy(tok_hbm, tok.at[0, :, own_rows], own_sem)
    own.start()
    for i in range(4):
        load_w1(i).start()
    load_bin = pltpu.make_async_copy(bin_hbm, bin_raw, bias_sem.at[0])
    load_bin.start()
    load_bout = pltpu.make_async_copy(bout_hbm, bout_raw, bias_sem.at[1])
    load_bout.start()
    load_w2 = pltpu.make_async_copy(w2_hbm, w2, w2_sem)

    pl.semaphore_wait(barrier, len(partners))

    def block(r):
        return tok.at[r, :, own_rows]

    def to_sibling(r):
        return remote(block(r), block(r), fwd_ss.at[r], fwd_rs.at[r], sibling)

    def from_sibling(r):
        return remote(tok.at[r, :, other_rows], tok.at[r, :, other_rows], fwd_ss.at[r], fwd_rs.at[r], sibling)

    own.wait()
    to_sibling(0).start()

    def to_low(u):
        return remote(tok.at[0, u, own_rows], tok.at[2, u, own_rows], low_ss.at[u], low_rs.at[u], low)

    for u in (0, 1):
        to_low(u).start()

    def along(side, d, u=None):
        src = 2 * side
        if d == 2:
            r = 6 - 2 * side
            return remote(block(src), block(r), z_ss.at[side, 4], tok_rs.at[r], along_z(2))
        r, i = ((1, 7), (3, 5))[side][u], d // 2
        return remote(tok.at[src, u, own_rows], tok.at[r, i, own_rows], z_ss.at[side, 2 * i + u], tok_rs.at[r], along_z(4 - d))

    along(0, 1, 0).start()
    along(0, 3, 0).start()

    def take(r):
        remote(block(r), block(r), fwd_ss.at[r], tok_rs.at[r], low).wait_recv()
        to_sibling(r).start()

    def pass_on(p):
        @pl.when(p == 1)
        def _():
            take(1)
            to_low(0).wait_recv()
            along(1, 1, 0).start()
            along(1, 3, 0).start()

        @pl.when((p > 1) & (p < GROUPS - 1))
        def _():
            take(p + 1)

        @pl.when(p == 2)
        def _():
            along(1, 1, 1).start()
            along(1, 3, 1).start()
            along(0, 2).start()

        @pl.when(p == 3)
        def _():
            along(0, 1, 1).start()
            along(0, 3, 1).start()

    def x1_copy(k, h):
        return remote(x1s.at[k, h], x1r.at[k, h], x1_ss.at[k, h], x1_rs.at[k, h], dest1[h])

    def first(r):
        from_sibling(r).wait_recv()
        tokens = tok[r].reshape(ROWS, D)

        @pl.when(r == 1)
        def _():
            load_w2.start()
            load_bin.wait()
            load_bout.wait()
            bias_in[...] = bin_raw[...].astype(F32).reshape(1, FF)
            bias_out[...] = bout_raw[...].astype(F32).reshape(1, D)

        for i in range(4):
            h = i % 2

            @pl.when(r == 0)
            def _():
                load_w1(i).wait()

            part = jnp.dot(tokens, w1[:, cols(w1_order[i], PAIR)], preferred_element_type=F32)
            for u in (0, 1):
                if i < 2:
                    x1s[2 * r + u, h] = code(part[u * SLOT : (u + 1) * SLOT], HIDDEN_SCALE)
                    x1_copy(2 * r + u, h).start()
                else:
                    keep[2 * r + u, h] = part[u * SLOT : (u + 1) * SLOT]

        @pl.when(r == 1)
        def _():
            to_low(1).wait_recv()
            to_sibling(2).start()
            along(1, 2).start()

    def y_copy(k, h):
        return remote(ys.at[k, h], yr.at[k, h], y_ss.at[k, h], y_rs.at[k, h], across)

    def sum_x(k):
        for h in (0, 1):
            x1_copy(k, h).wait_recv()
            ys[k, h] = code(keep[k, h, other_half] + decode(x1r[k, h, other_half], HIDDEN_SCALE), HIDDEN_SCALE)
            y_copy(k, h).start()
        for h in (0, 1):
            keep[k, h, my_half] += decode(x1r[k, h, my_half], HIDDEN_SCALE)

    def x2_copy(k, h):
        return remote(x2s.at[k, h], x2r.at[k, h], x2_ss.at[k, h], x2_rs.at[k, h], dest2[h])

    def sum_y(k):
        for h in (0, 1):
            y_copy(k, h).wait_recv()
            x2s[k, h] = code(keep[k, h, my_half, gone[h]] + decode(yr[k, h, :, gone[h]], HIDDEN_SCALE), HIDDEN_SCALE)
            x2_copy(k, h).start()
        for h in (0, 1):
            keep[k, h, my_half, kept[h]] += decode(yr[k, h, :, kept[h]], HIDDEN_SCALE)

    def hid_copy(k, which, start, size, ss, rs, dev):
        c = cols(start, size)
        return remote(hid.at[k, which, c], hid.at[k, which, c], ss, rs, dev)

    def gx_copy(k, h):
        return hid_copy(k, my_half, quarter_of[h], QUARTER, gx_ss.at[k, h], gx_rs.at[k, h], dest2[h])

    def gy_copy(k, h):
        return hid_copy(k, my_half, pair_of[h], PAIR, gy_ss.at[k, h], gy_rs.at[k, h], across)

    def gxx_copy(k, h):
        return hid_copy(k, pl.ds(0, SLOT), pair_of[h], PAIR, gxx_ss.at[k, h], gxx_rs.at[k, h], dest1[h])

    def activate(k):
        for h in (0, 1):
            x2_copy(k, h).wait_recv()
            c = cols(quarter_of[h], QUARTER)
            summed = keep[k, h, my_half, kept[h]] + decode(x2r[k, h], HIDDEN_SCALE)
            hid[k, my_half, c] = jax.nn.gelu(summed + bias_in[:, c], approximate=True).astype(BF16)
            gx_copy(k, h).start()

    def gather_y(k):
        for h in (0, 1):
            gx_copy(k, h).wait_recv()
            gy_copy(k, h).start()

    def gather_x(k):
        for h in (0, 1):
            gy_copy(k, h).wait_recv()
            gxx_copy(k, h).start()
        for h in (0, 1):
            x1_copy(k, h).wait_send()
            y_copy(k, h).wait_send()
            x2_copy(k, h).wait_send()

    def c_copy(m, i):
        r, c = (m + 1) % GROUPS, pl.ds(i * PAIR, PAIR)
        return remote(po.at[m % 2, :, other_rows, c], cr.at[r, :, :, c], c_ss.at[m % 2, i], c_rs.at[r, i], sibling)

    def second(m):
        r = (m + 1) % GROUPS

        @pl.when(m == 0)
        def _():
            load_w2.wait()

        @pl.when(m >= 2)
        def _():
            for i in (0, 1):
                c_copy(m - 2, i).wait_send()

        for u in (0, 1):
            for h in (0, 1):
                gxx_copy(2 * r + u, h).wait_recv()
        hidden = hid[pl.ds(2 * r, 2)].reshape(ROWS, FF)
        for i in (0, 1):
            c = pl.ds(i * PAIR, PAIR)
            po[m % 2, :, :, c] = jnp.dot(hidden, w2[:, c], preferred_element_type=F32).reshape(2, SLOT, PAIR)
            c_copy(m, i).start()
        for u in (0, 1):
            for h in (0, 1):
                gx_copy(2 * r + u, h).wait_send()
                gy_copy(2 * r + u, h).wait_send()

    def o_copy(m, u):
        r = (m + 1) % GROUPS
        d = 2 + r % 2 * (2 * u - 1)
        return remote(osend.at[m % 2, u], orecv.at[r, u], o_ss.at[m % 2, u], o_rs.at[r, u], along_z(d))

    def send_out(m):
        r = (m + 1) % GROUPS
        for i in (0, 1):
            c_copy(m, i).wait_recv()

        @pl.when((m == 1) | (m == 7))
        def _():
            acc[m // 4] = po[m % 2, :, own_rows] + cr[r]

        @pl.when((m != 1) & (m != 7))
        def _():
            for u in (0, 1):
                @pl.when(m == 2)
                def _():
                    o_copy(0, u).wait_send()

                @pl.when(m >= 4)
                def _():
                    o_copy(m - 2, u).wait_send()

                osend[m % 2, u] = code(po[m % 2, u, own_rows] + cr[r, u], OUT_SCALE)
                o_copy(m, u).start()

        to_sibling(r).wait_send()
        for u in (0, 1):
            for h in (0, 1):
                gxx_copy(2 * r + u, h).wait_send()

    def y2_copy(u):
        return remote(y2s.at[u], y2r.at[u], y2_ss.at[u], y2_rs.at[u], low)

    def others(u, a, b, c):
        r = c if u else a
        for i in (0, 1):
            o_copy(r - 1, i).wait_recv()
        o_copy(b - 1, u).wait_recv()
        return decode(orecv[r, 0], OUT_SCALE) + decode(orecv[r, 1], OUT_SCALE) + decode(orecv[b, u], OUT_SCALE)

    def cross(m):
        for u in (0, 1):
            @pl.when(m == 3 + u)
            def _():
                y2s[u] = code(acc[0, u] + others(u, 3, 4, 5), OUT_SCALE)
                y2_copy(u).start()

        @pl.when(m == 4)
        def _():
            for u in (0, 1):
                to_low(u).wait_send()
            for side in (0, 1):
                for d in (1, 3):
                    for u in (0, 1):
                        along(side, d, u).wait_send()
                along(side, 2).wait_send()

    tasks = dict(first=first, pass_on=pass_on, sum_x=sum_x, sum_y=sum_y, activate=activate, gather_y=gather_y,
                 gather_x=gather_x, second=second, send_out=send_out, cross=cross)

    def step(s, _):
        for name, lag in ORDER:
            p = s - lag

            @pl.when((p >= 0) & (p < GROUPS))
            def _():
                if name[-1] in "01":
                    r = (p + 1) % GROUPS if name.startswith("gather") else p
                    tasks[name[:-1]](2 * r + int(name[-1]))
                else:
                    tasks[name](p)

        return 0

    lax.fori_loop(0, STEPS, step, 0)

    for u in (0, 1):
        y2_copy(u).wait_recv()
        rest = acc[1, u] + decode(y2r[u], OUT_SCALE) + bias_out[...]
        out_ref[u] = rest + others(u, 1, 6, 7)

    for i in (0, 1):
        for m in (GROUPS - 2, GROUPS - 1):
            c_copy(m, i).wait_send()
        for m in (5, 6):
            o_copy(m, i).wait_send()
    for u in (0, 1):
        y2_copy(u).wait_send()


def per_device(tokens, w_in, b_in, w_out, b_out):
    any_space, vmem = pl.BlockSpec(memory_space=pl.ANY), pl.BlockSpec(memory_space=pltpu.VMEM)
    dma = pltpu.SemaphoreType.DMA
    g, n = GROUPS, SLOTS
    scratch = [
        pltpu.VMEM((D, FF), BF16), pltpu.VMEM((FF, D), BF16), pltpu.VMEM((FF,), BF16), pltpu.VMEM((D,), BF16), pltpu.VMEM((1, FF), F32), pltpu.VMEM((1, D), F32), pltpu.VMEM((g, 2, SLOT, D), BF16),
        pltpu.VMEM((n, 2, SLOT, PAIR), BF16), pltpu.VMEM((n, 2, SLOT, PAIR), BF16), pltpu.VMEM((n, 2, SLOT, PAIR), F32),
        pltpu.VMEM((n, 2, HALF, PAIR), BF16), pltpu.VMEM((n, 2, HALF, PAIR), BF16),
        pltpu.VMEM((n, 2, HALF, QUARTER), BF16), pltpu.VMEM((n, 2, HALF, QUARTER), BF16),
        pltpu.VMEM((n, SLOT, FF), BF16), pltpu.VMEM((2, 2, SLOT, D), F32), pltpu.VMEM((g, 2, HALF, D), F32),
        pltpu.VMEM((2, 2, HALF, D), BF16), pltpu.VMEM((g, 2, HALF, D), BF16), pltpu.VMEM((2, 2, HALF, D), F32),
        pltpu.VMEM((2, HALF, D), BF16), pltpu.VMEM((2, HALF, D), BF16),
        dma((4,)), dma, dma((2,)), dma, dma((2,)), dma((2,)), dma((g,)), dma((2, 5)), dma((g,)), dma((g,)),
        dma((n, 2)), dma((n, 2)), dma((n, 2)), dma((n, 2)), dma((n, 2)), dma((n, 2)),
        dma((n, 2)), dma((n, 2)), dma((n, 2)), dma((n, 2)), dma((n, 2)), dma((n, 2)),
        dma((2, 2)), dma((g, 2)), dma((2, 2)), dma((g, 2)), dma((2,)), dma((2,)),
    ]
    out = pl.pallas_call(
        kernel,
        out_shape=pltpu.VMEM((2, HALF, D), F32),
        in_specs=[any_space] * 5,
        out_specs=vmem,
        scratch_shapes=scratch,
        compiler_params=pltpu.CompilerParams(collective_id=0, has_side_effects=True, vmem_limit_bytes=62 * 2**20),
        cost_estimate=pl.CostEstimate(flops=4 * 1024 * D * FF, bytes_accessed=4 * D * FF, transcendentals=1024 * QUARTER),
    )(tokens.reshape(2, HALF, D), w_in, b_in, w_out, b_out)
    return out.reshape(2 * HALF, D)


def solution(mesh):
    return jax.shard_map(
        per_device,
        mesh=mesh,
        in_specs=(P("col", "row"), P("row", "col"), P("col"), P("col", "row"), P("row")),
        out_specs=P("col", "row"),
        check_vma=False,
    )
```

```python
import jax
import jax.numpy as jnp
from jax import lax
from jax.experimental import pallas as pl
from jax.experimental.pallas import tpu as pltpu
from jax.sharding import PartitionSpec as P

MESH = pl.DeviceIdType.MESH
F32, BF16 = jnp.float32, jnp.bfloat16
GROUPS, SLOTS = 8, 16
ROWS, SLOT, HALF = 128, 64, 32
D, FF = 1536, 3072
PAIR, QUARTER = 768, 384

HIDDEN_SCALE, OUT_SCALE = 2.0**20, 2.0**9

ORDER = (
    ("gather_y0", 6), ("first", 0), ("gather_x0", 8), ("sum_x0", 1), ("second", 10), ("sum_y1", 3), ("activate1", 4),
    ("gather_x1", 8), ("cross", 12), ("sum_x1", 1), ("sum_y0", 2), ("send_out", 10), ("pass_on", -1),
    ("activate0", 3), ("gather_y1", 6),
)
STEPS = 18


def code(v, scale):
    v = v * scale
    return ((v * v) * (v * jnp.abs(v))).astype(BF16)


def decode(coded, scale):
    y = coded.astype(F32)
    r = lax.rsqrt(jnp.maximum(jnp.abs(y), 1e-37))
    return y * (r * r) * (lax.rsqrt(r) * (1.0 / scale))


def kernel(tok_hbm, w1_hbm, bin_hbm, w2_hbm, bout_hbm, out_ref,
           w1, w2, bin_raw, bout_raw, bias_in, bias_out, tok, x1s, x1r, keep, ys, yr, x2s, x2r, hid, po, cr, osend, orecv, acc, y2s, y2r,
           w1_sem, w2_sem, bias_sem, own_sem, low_ss, low_rs, tok_rs, z_ss, fwd_ss, fwd_rs,
           x1_ss, x1_rs, y_ss, y_rs, x2_ss, x2_rs, gx_ss, gx_rs, gy_ss, gy_rs, gxx_ss, gxx_rs,
           c_ss, c_rs, o_ss, o_rs, y2_ss, y2_rs):
    row, col = lax.axis_index("row"), lax.axis_index("col")
    x, yh = row // 2, row % 2
    yl, z, core = col // 8, (col // 2) % 4, col % 2
    x_one = x + 1 - 2 * (x % 2)
    x_three = 3 - x
    one = (x_one * 2 + yh, col)
    three = (x_three * 2 + yh, col)
    across = (x * 2 + 1 - yh, col)
    sibling = (row, col + 1 - 2 * core)
    low = (row, (1 - yl) * 8 + z * 2 + core)

    def along_z(d):
        return (row, yl * 8 + ((z + d) % 4) * 2 + core)

    def cols(start, size):
        return pl.ds(pl.multiple_of(start, 128), size)

    def rows(start, size=HALF):
        return pl.ds(pl.multiple_of(start, HALF), size)

    mine = (((x + 1) // 2) % 2, x // 2)
    q = (x // 2, x % 2)
    pair_of = tuple(h * 2 * PAIR + mine[h] * PAIR for h in (0, 1))
    other_pair = tuple(h * 2 * PAIR + (1 - mine[h]) * PAIR for h in (0, 1))
    quarter_of = tuple(pair_of[h] + q[h] * QUARTER for h in (0, 1))
    kept = tuple(cols(q[h] * QUARTER, QUARTER) for h in (0, 1))
    gone = tuple(cols((1 - q[h]) * QUARTER, QUARTER) for h in (0, 1))
    dest1, dest2 = (one, three), (three, one)
    my_half, other_half = rows(yh * HALF), rows((1 - yh) * HALF)
    own_rows, other_rows = rows(core * HALF), rows((1 - core) * HALF)

    def remote(src, dst, ss, rs, dev):
        return pltpu.make_async_remote_copy(src_ref=src, dst_ref=dst, send_sem=ss, recv_sem=rs, device_id=dev, device_id_type=MESH)

    barrier = pltpu.get_barrier_semaphore()
    partners = [one, three, across, sibling, low] + [along_z(d) for d in (1, 2, 3)]
    for dev in partners:
        pl.semaphore_signal(barrier, inc=1, device_id=dev, device_id_type=MESH)

    w1_order = (other_pair[0], other_pair[1], pair_of[0], pair_of[1])

    def load_w1(i):
        c = cols(w1_order[i], PAIR)
        return pltpu.make_async_copy(w1_hbm.at[:, c], w1.at[:, c], w1_sem.at[i])

    own = pltpu.make_async_copy(tok_hbm, tok.at[0, :, own_rows], own_sem)
    own.start()
    for i in range(4):
        load_w1(i).start()
    load_bin = pltpu.make_async_copy(bin_hbm, bin_raw, bias_sem.at[0])
    load_bin.start()
    load_bout = pltpu.make_async_copy(bout_hbm, bout_raw, bias_sem.at[1])
    load_bout.start()
    load_w2 = pltpu.make_async_copy(w2_hbm, w2, w2_sem)

    pl.semaphore_wait(barrier, len(partners))

    def block(r):
        return tok.at[r, :, own_rows]

    def to_sibling(r):
        return remote(block(r), block(r), fwd_ss.at[r], fwd_rs.at[r], sibling)

    def from_sibling(r):
        return remote(tok.at[r, :, other_rows], tok.at[r, :, other_rows], fwd_ss.at[r], fwd_rs.at[r], sibling)

    own.wait()
    to_sibling(0).start()

    def to_low(u):
        return remote(tok.at[0, u, own_rows], tok.at[2, u, own_rows], low_ss.at[u], low_rs.at[u], low)

    for u in (0, 1):
        to_low(u).start()

    def along(side, d, u=None):
        src = 2 * side
        if d == 2:
            r = 6 - 2 * side
            return remote(block(src), block(r), z_ss.at[side, 4], tok_rs.at[r], along_z(2))
        r, i = ((1, 7), (3, 5))[side][u], d // 2
        return remote(tok.at[src, u, own_rows], tok.at[r, i, own_rows], z_ss.at[side, 2 * i + u], tok_rs.at[r], along_z(4 - d))

    along(0, 1, 0).start()
    along(0, 3, 0).start()

    def take(r):
        remote(block(r), block(r), fwd_ss.at[r], tok_rs.at[r], low).wait_recv()
        to_sibling(r).start()

    def pass_on(p):
        @pl.when(p == 1)
        def _():
            take(1)
            to_low(0).wait_recv()
            along(1, 1, 0).start()
            along(1, 3, 0).start()

        @pl.when((p > 1) & (p < GROUPS - 1))
        def _():
            take(p + 1)

        @pl.when(p == 2)
        def _():
            along(1, 1, 1).start()
            along(1, 3, 1).start()
            along(0, 2).start()

        @pl.when(p == 3)
        def _():
            along(0, 1, 1).start()
            along(0, 3, 1).start()

    def x1_copy(k, h):
        return remote(x1s.at[k, h], x1r.at[k, h], x1_ss.at[k, h], x1_rs.at[k, h], dest1[h])

    def first(r):
        from_sibling(r).wait_recv()
        tokens = tok[r].reshape(ROWS, D)

        @pl.when(r == 1)
        def _():
            load_w2.start()
            load_bin.wait()
            load_bout.wait()
            bias_in[...] = bin_raw[...].astype(F32).reshape(1, FF)
            bias_out[...] = bout_raw[...].astype(F32).reshape(1, D)

        for i in range(4):
            h = i % 2

            @pl.when(r == 0)
            def _():
                load_w1(i).wait()

            part = jnp.dot(tokens, w1[:, cols(w1_order[i], PAIR)], preferred_element_type=F32)
            for u in (0, 1):
                if i < 2:
                    x1s[2 * r + u, h] = code(part[u * SLOT : (u + 1) * SLOT], HIDDEN_SCALE)
                    x1_copy(2 * r + u, h).start()
                else:
                    keep[2 * r + u, h] = part[u * SLOT : (u + 1) * SLOT]

        @pl.when(r == 1)
        def _():
            to_low(1).wait_recv()
            to_sibling(2).start()
            along(1, 2).start()

    def y_copy(k, h):
        return remote(ys.at[k, h], yr.at[k, h], y_ss.at[k, h], y_rs.at[k, h], across)

    def sum_x(k):
        for h in (0, 1):
            x1_copy(k, h).wait_recv()
            ys[k, h] = code(keep[k, h, other_half] + decode(x1r[k, h, other_half], HIDDEN_SCALE), HIDDEN_SCALE)
            y_copy(k, h).start()
        for h in (0, 1):
            keep[k, h, my_half] += decode(x1r[k, h, my_half], HIDDEN_SCALE)

    def x2_copy(k, h):
        return remote(x2s.at[k, h], x2r.at[k, h], x2_ss.at[k, h], x2_rs.at[k, h], dest2[h])

    def sum_y(k):
        for h in (0, 1):
            y_copy(k, h).wait_recv()
            x2s[k, h] = code(keep[k, h, my_half, gone[h]] + decode(yr[k, h, :, gone[h]], HIDDEN_SCALE), HIDDEN_SCALE)
            x2_copy(k, h).start()
        for h in (0, 1):
            keep[k, h, my_half, kept[h]] += decode(yr[k, h, :, kept[h]], HIDDEN_SCALE)

    def hid_copy(k, which, start, size, ss, rs, dev):
        c = cols(start, size)
        return remote(hid.at[k, which, c], hid.at[k, which, c], ss, rs, dev)

    def gx_copy(k, h):
        return hid_copy(k, my_half, quarter_of[h], QUARTER, gx_ss.at[k, h], gx_rs.at[k, h], dest2[h])

    def gy_copy(k, h):
        return hid_copy(k, my_half, pair_of[h], PAIR, gy_ss.at[k, h], gy_rs.at[k, h], across)

    def gxx_copy(k, h):
        return hid_copy(k, pl.ds(0, SLOT), pair_of[h], PAIR, gxx_ss.at[k, h], gxx_rs.at[k, h], dest1[h])

    def activate(k):
        for h in (0, 1):
            x2_copy(k, h).wait_recv()
            c = cols(quarter_of[h], QUARTER)
            summed = keep[k, h, my_half, kept[h]] + decode(x2r[k, h], HIDDEN_SCALE)
            hid[k, my_half, c] = jax.nn.gelu(summed + bias_in[:, c], approximate=True).astype(BF16)
            gx_copy(k, h).start()

    def gather_y(k):
        for h in (0, 1):
            gx_copy(k, h).wait_recv()
            gy_copy(k, h).start()

    def gather_x(k):
        for h in (0, 1):
            gy_copy(k, h).wait_recv()
            gxx_copy(k, h).start()
        for h in (0, 1):
            x1_copy(k, h).wait_send()
            y_copy(k, h).wait_send()
            x2_copy(k, h).wait_send()

    def c_copy(m, i):
        r, c = (m + 1) % GROUPS, pl.ds(i * PAIR, PAIR)
        return remote(po.at[m % 2, :, other_rows, c], cr.at[r, :, :, c], c_ss.at[m % 2, i], c_rs.at[r, i], sibling)

    def second(m):
        r = (m + 1) % GROUPS

        @pl.when(m == 0)
        def _():
            load_w2.wait()

        @pl.when(m >= 2)
        def _():
            for i in (0, 1):
                c_copy(m - 2, i).wait_send()

        def product(pairs, c):
            return sum(
                jnp.dot(hid[pl.ds(2 * r, 2), :, cols(p, PAIR)].reshape(ROWS, PAIR), w2[cols(p, PAIR), c], preferred_element_type=F32)
                for p in pairs
            ).reshape(2, SLOT, PAIR)

        for i in (0, 1):
            c = pl.ds(i * PAIR, PAIR)
            po[m % 2, :, :, c] = product(pair_of, c)
        for u in (0, 1):
            for h in (0, 1):
                gxx_copy(2 * r + u, h).wait_recv()
        for i in (0, 1):
            c = pl.ds(i * PAIR, PAIR)
            po[m % 2, :, :, c] += product(other_pair, c)
            c_copy(m, i).start()
        for u in (0, 1):
            for h in (0, 1):
                gx_copy(2 * r + u, h).wait_send()
                gy_copy(2 * r + u, h).wait_send()

    def o_copy(m, u):
        r = (m + 1) % GROUPS
        d = 2 + r % 2 * (2 * u - 1)
        return remote(osend.at[m % 2, u], orecv.at[r, u], o_ss.at[m % 2, u], o_rs.at[r, u], along_z(d))

    def send_out(m):
        r = (m + 1) % GROUPS
        for i in (0, 1):
            c_copy(m, i).wait_recv()

        @pl.when((m == 1) | (m == 7))
        def _():
            acc[m // 4] = po[m % 2, :, own_rows] + cr[r]

        @pl.when((m != 1) & (m != 7))
        def _():
            for u in (0, 1):
                @pl.when(m == 2)
                def _():
                    o_copy(0, u).wait_send()

                @pl.when(m >= 4)
                def _():
                    o_copy(m - 2, u).wait_send()

                osend[m % 2, u] = code(po[m % 2, u, own_rows] + cr[r, u], OUT_SCALE)
                o_copy(m, u).start()

        to_sibling(r).wait_send()
        for u in (0, 1):
            for h in (0, 1):
                gxx_copy(2 * r + u, h).wait_send()

    def y2_copy(u):
        return remote(y2s.at[u], y2r.at[u], y2_ss.at[u], y2_rs.at[u], low)

    def others(u, a, b, c):
        r = c if u else a
        for i in (0, 1):
            o_copy(r - 1, i).wait_recv()
        o_copy(b - 1, u).wait_recv()
        return decode(orecv[r, 0], OUT_SCALE) + decode(orecv[r, 1], OUT_SCALE) + decode(orecv[b, u], OUT_SCALE)

    def cross(m):
        for u in (0, 1):
            @pl.when(m == 3 + u)
            def _():
                y2s[u] = code(acc[0, u] + others(u, 3, 4, 5), OUT_SCALE)
                y2_copy(u).start()

        @pl.when(m == 4)
        def _():
            for u in (0, 1):
                to_low(u).wait_send()
            for side in (0, 1):
                for d in (1, 3):
                    for u in (0, 1):
                        along(side, d, u).wait_send()
                along(side, 2).wait_send()

    tasks = dict(first=first, pass_on=pass_on, sum_x=sum_x, sum_y=sum_y, activate=activate, gather_y=gather_y,
                 gather_x=gather_x, second=second, send_out=send_out, cross=cross)

    def step(s, _):
        for name, lag in ORDER:
            p = s - lag

            @pl.when((p >= 0) & (p < GROUPS))
            def _():
                if name[-1] in "01":
                    r = (p + 1) % GROUPS if name.startswith("gather") else p
                    tasks[name[:-1]](2 * r + int(name[-1]))
                else:
                    tasks[name](p)

        return 0

    lax.fori_loop(0, STEPS, step, 0)

    for u in (0, 1):
        y2_copy(u).wait_recv()
        rest = acc[1, u] + decode(y2r[u], OUT_SCALE) + bias_out[...]
        out_ref[u] = rest + others(u, 1, 6, 7)

    for i in (0, 1):
        for m in (GROUPS - 2, GROUPS - 1):
            c_copy(m, i).wait_send()
        for m in (5, 6):
            o_copy(m, i).wait_send()
    for u in (0, 1):
        y2_copy(u).wait_send()


def per_device(tokens, w_in, b_in, w_out, b_out):
    any_space, vmem = pl.BlockSpec(memory_space=pl.ANY), pl.BlockSpec(memory_space=pltpu.VMEM)
    dma = pltpu.SemaphoreType.DMA
    g, n = GROUPS, SLOTS
    scratch = [
        pltpu.VMEM((D, FF), BF16), pltpu.VMEM((FF, D), BF16), pltpu.VMEM((FF,), BF16), pltpu.VMEM((D,), BF16), pltpu.VMEM((1, FF), F32), pltpu.VMEM((1, D), F32), pltpu.VMEM((g, 2, SLOT, D), BF16),
        pltpu.VMEM((n, 2, SLOT, PAIR), BF16), pltpu.VMEM((n, 2, SLOT, PAIR), BF16), pltpu.VMEM((n, 2, SLOT, PAIR), F32),
        pltpu.VMEM((n, 2, HALF, PAIR), BF16), pltpu.VMEM((n, 2, HALF, PAIR), BF16),
        pltpu.VMEM((n, 2, HALF, QUARTER), BF16), pltpu.VMEM((n, 2, HALF, QUARTER), BF16),
        pltpu.VMEM((n, SLOT, FF), BF16), pltpu.VMEM((2, 2, SLOT, D), F32), pltpu.VMEM((g, 2, HALF, D), F32),
        pltpu.VMEM((2, 2, HALF, D), BF16), pltpu.VMEM((g, 2, HALF, D), BF16), pltpu.VMEM((2, 2, HALF, D), F32),
        pltpu.VMEM((2, HALF, D), BF16), pltpu.VMEM((2, HALF, D), BF16),
        dma((4,)), dma, dma((2,)), dma, dma((2,)), dma((2,)), dma((g,)), dma((2, 5)), dma((g,)), dma((g,)),
        dma((n, 2)), dma((n, 2)), dma((n, 2)), dma((n, 2)), dma((n, 2)), dma((n, 2)),
        dma((n, 2)), dma((n, 2)), dma((n, 2)), dma((n, 2)), dma((n, 2)), dma((n, 2)),
        dma((2, 2)), dma((g, 2)), dma((2, 2)), dma((g, 2)), dma((2,)), dma((2,)),
    ]
    out = pl.pallas_call(
        kernel,
        out_shape=pltpu.VMEM((2, HALF, D), F32),
        in_specs=[any_space] * 5,
        out_specs=vmem,
        scratch_shapes=scratch,
        compiler_params=pltpu.CompilerParams(collective_id=0, has_side_effects=True, vmem_limit_bytes=62 * 2**20),
        cost_estimate=pl.CostEstimate(flops=4 * 1024 * D * FF, bytes_accessed=4 * D * FF, transcendentals=1024 * QUARTER),
    )(tokens.reshape(2, HALF, D), w_in, b_in, w_out, b_out)
    return out.reshape(2 * HALF, D)


def solution(mesh):
    return jax.shard_map(
        per_device,
        mesh=mesh,
        in_specs=(P("col", "row"), P("row", "col"), P("col"), P("col", "row"), P("row")),
        out_specs=P("col", "row"),
        check_vma=False,
    )
```
